512 devices in a mesh: clu: 128 (over z, y, core), head: 4 (over x).
Axes of the slice: x: 4, y: 4, z: 16, core: 2. Of those that a mesh axis runs over, the one named last changes fastest.
Arguments:
- query: bfloat16 [40960, 3072], P('clu', 'head'), may hold values from -200 to 200
- key: bfloat16 [40960, 3072], P('clu', 'head'), may hold values from -6.1 to 6.1
- value: bfloat16 [40960, 3072], P('clu', 'head'), may hold values from -6 to 6
- labels: int32 [40960], P('clu'), may hold values from 0 to 2559, as said below
- partners: int32 [2560, 3], replicated, may hold values from 0 to 2559, as said below
- out_weight: bfloat16 [3072, 3072], P('head', 'clu'), may hold values from -0.109375 to 0.109375
Outputs:
- mixed: bfloat16 [40960, 3072], P('clu', 'head')
The draws below stay inside these ranges and needn't reach their ends.
Inputs may be any that keep to these rules, and one draw needn't show every extreme that they name: Every cluster has exactly 16 tokens. Among the 320 tokens of one aligned block, at most 4 have labels in any one group of 20 consecutive clusters (same labels // 20), and some group reaches 4 in every block. For the 20 clusters of one group (same g // 20), all their listed partners are distinct and lie outside that group, and at most 1 of them lie in any one other group, a bound that some other group reaches for every group.
All inputs are finite; a program needn't handle non-finite values.
Results may differ from the reference program's by a relative error of at most 0.013.
Values may be sent and summed in bfloat16 or wider, within the bound.
A program may use at most 128 MiB of HBM per device.

```python
import math
import jax
import jax.numpy as jnp
from jax import lax

HEADS = 24
HD = 128
D_OUT = 3072
TOK_DEV = 320
CSIZE = 16
P_SIZE = 3
CL_DEV = 20
TOKENS = 40960
CLUSTERS = 2560
QCAP = 4
CAP = 1
N_CLU = 128
N_HEAD = 4


def cluster_labels(key):
    key = jax.random.fold_in(key, 101)
    subkeys = jax.random.split(key, 4)
    slot_count = N_CLU * QCAP
    scores = jax.random.permutation(subkeys[0], slot_count).astype(jnp.int32)
    forced = jax.random.randint(subkeys[1], (), 0, N_CLU)
    slot_owner = jnp.arange(slot_count, dtype=jnp.int32) // QCAP
    scores = jnp.where(slot_owner == forced, scores - slot_count, scores)
    chosen = jnp.argsort(scores)[:TOK_DEV].astype(jnp.int32)
    shifts = chosen // QCAP
    sources = jnp.arange(N_CLU, dtype=jnp.int32)
    owners = (sources[:, None] + shifts[None, :]) % N_CLU
    within = jax.vmap(lambda subkey: jax.random.permutation(subkey, TOK_DEV))(jax.random.split(subkeys[2], N_CLU)).astype(jnp.int32)
    places = jax.vmap(lambda subkey: jax.random.permutation(subkey, TOK_DEV))(jax.random.split(subkeys[3], N_CLU)).astype(jnp.int32)
    columns = jnp.arange(TOK_DEV, dtype=jnp.int32)[None, :]
    cluster = owners * CL_DEV + within[owners, columns] // CSIZE
    placed = jax.vmap(lambda place, label: jnp.zeros((TOK_DEV,), jnp.int32).at[place].set(label))(places, cluster)
    return placed.reshape(TOKENS)


def key_field(key):
    key = jax.random.fold_in(key, 202)
    return jnp.clip(jax.random.normal(key, (TOKENS, HEADS * HD), jnp.float32), -6.0, 6.0)


def draw_labels(key, part):
    return cluster_labels(key)


def draw_partners(key, part):
    key = jax.random.fold_in(key, 7)
    slot_count = N_CLU * CAP
    entries = CL_DEV * P_SIZE

    def for_owner(subkey, owner):
        subkeys = jax.random.split(subkey, 4)
        scores = jax.random.permutation(subkeys[0], slot_count).astype(jnp.int32)
        chosen_owner = (owner + 1 + jax.random.randint(subkeys[1], (), 0, N_CLU - 1)) % N_CLU
        slot_owner = jnp.arange(slot_count, dtype=jnp.int32) // CAP
        scores = jnp.where(slot_owner == chosen_owner, scores - slot_count, scores)
        scores = jnp.where(slot_owner == owner, scores + slot_count, scores)
        picked = jnp.argsort(scores)[:entries].astype(jnp.int32)
        source = picked // CAP
        inside = picked % CAP
        offsets = jax.random.randint(subkeys[2], (N_CLU,), 0, CL_DEV)
        cluster = source * CL_DEV + (inside + offsets[source]) % CL_DEV
        shuffle = jax.random.permutation(subkeys[3], entries)
        return cluster[shuffle].reshape(CL_DEV, P_SIZE)
    lists = jax.vmap(for_owner)(jax.random.split(key, N_CLU), jnp.arange(N_CLU, dtype=jnp.int32))
    return lists.reshape(CLUSTERS, P_SIZE).astype(jnp.int32)


def draw_key(key, part):
    field = key_field(key)
    return field.astype(jnp.bfloat16)


def draw_query(key, part):
    key = jax.random.fold_in(key, 303)
    field = jnp.clip(jax.random.normal(key, (TOKENS, HEADS * HD), jnp.float32), -6.0, 6.0)
    return field.astype(jnp.bfloat16)


def shard_levels(key, shape, cuts, least, top_value):
    def one(axis_at, shards_of):
        draws = jax.random.uniform(jax.random.fold_in(jax.random.fold_in(key, 6), axis_at), (shards_of,), jnp.float32, least / len(cuts), top_value / len(cuts))
        return jnp.repeat(jnp.exp(draws), shape[axis_at] // shards_of).reshape((-1,) + (1,) * (len(shape) - axis_at - 1))

    gain = one(*cuts[0])
    for cut in cuts[1:]:
        gain = gain * one(*cut)
    return gain


def gaussian(rng, shape, deviation, bound, cuts=(), held_as=jnp.bfloat16):
    values = deviation * jax.random.normal(rng, shape, jnp.float32)
    if cuts:
        values = values * shard_levels(rng, shape, cuts, -0.22, 0.18)
    return jnp.clip(values, -bound, bound).astype(held_as)


def setup_inputs(seed: int = 0) -> dict:
    seeds = jax.random.split(jax.random.key(seed), 7)
    return {
        "query": draw_query(jax.random.fold_in(seeds[6], 71), 0),
        "key": draw_key(jax.random.fold_in(seeds[6], 71), 0),
        "value": gaussian(seeds[2], (TOKENS, HEADS * HD), 1.0, 6.0, ((0, 128), (1, 4))),
        "labels": draw_labels(jax.random.fold_in(seeds[6], 71), 0),
        "partners": draw_partners(jax.random.fold_in(seeds[6], 71), 0),
        "out_weight": gaussian(seeds[5], (HEADS * HD, D_OUT), (HEADS * HD) ** -0.5, 0.109375, ((0, 4), (1, 128))),
    }


def reference(query, key, value, labels, partners, out_weight):
    order = jnp.argsort(labels, stable=True).astype(jnp.int32)
    query_grouped = query[order].reshape(CLUSTERS, CSIZE, HEADS, HD)
    key_grouped = key[order].reshape(CLUSTERS, CSIZE, HEADS, HD)
    value_grouped = value[order].reshape(CLUSTERS, CSIZE, HEADS, HD)
    scale = 1.0 / math.sqrt(HD)
    block_size = math.gcd(CLUSTERS, 64)

    def attend(start):
        own_query = lax.dynamic_slice_in_dim(query_grouped, start, block_size, 0)
        own_key = lax.dynamic_slice_in_dim(key_grouped, start, block_size, 0)
        own_value = lax.dynamic_slice_in_dim(value_grouped, start, block_size, 0)
        listed = lax.dynamic_slice_in_dim(partners, start, block_size, 0)
        far_key = key_grouped[listed].reshape(block_size, P_SIZE * CSIZE, HEADS, HD)
        far_value = value_grouped[listed].reshape(block_size, P_SIZE * CSIZE, HEADS, HD)
        all_key = jnp.concatenate([own_key, far_key], axis=1).astype(jnp.float32)
        all_value = jnp.concatenate([own_value, far_value], axis=1).astype(jnp.float32)
        scores = jnp.einsum('cqhd,ckhd->chqk', own_query.astype(jnp.float32), all_key) * scale
        highest = lax.optimization_barrier(jnp.max(scores, axis=-1, keepdims=True))
        powers = jnp.exp(scores - highest)
        weights = (powers / lax.optimization_barrier(jnp.sum(powers, axis=-1, keepdims=True))).astype(jnp.bfloat16)
        result = jnp.einsum('chqk,ckhd->cqhd', weights.astype(jnp.float32), all_value)
        return result.astype(jnp.bfloat16)
    starts = jnp.arange(CLUSTERS // block_size, dtype=jnp.int32) * block_size
    blocks = lax.map(attend, starts)
    grouped_out = blocks.reshape(TOKENS, HEADS * HD)
    attended = jnp.zeros_like(query).at[order].set(grouped_out)
    group_width = HEADS // N_HEAD * HD
    total = jnp.zeros((TOKENS, D_OUT), jnp.float32)
    for group in range(N_HEAD):
        lower = group * group_width
        partial_value = jnp.dot(attended[:, lower:lower + group_width], out_weight[lower:lower + group_width], preferred_element_type=jnp.float32).astype(jnp.bfloat16)
        partial_value = lax.optimization_barrier(partial_value)
        total = total + partial_value.astype(jnp.float32)
    return total.astype(jnp.bfloat16)
```

```python
import functools
import math

import jax
import jax.numpy as jnp
from jax import lax
from jax.experimental import pallas as pl
from jax.experimental.pallas import tpu as pltpu
from jax.sharding import PartitionSpec as P

HD = 128
CSIZE = 16
PLANE = 8
SUBS = 4
MESH = pl.DeviceIdType.MESH
F32 = jnp.float32
BF16 = jnp.bfloat16


def ring_kernel(planes, pick_ref, kv_ref, out_ref, *rest):
    half = planes // 2
    ups = (kv_ref,) + rest[: half - 1]
    downs = (kv_ref,) + rest[half - 1 : 2 * half - 2]
    last = rest[2 * half - 2]
    stage, up_send, down_send, ring_recv, side_send, side_recv = rest[2 * half - 1 :]
    me = lax.axis_index("clu")
    z, i = me // PLANE, me % PLANE
    above = lax.rem(z + 1, planes) * PLANE + i
    below = lax.rem(z + planes - 1, planes) * PLANE + i
    step = kv_ref.shape[0] // SUBS

    def peer(j):
        return z * PLANE + lax.rem(i + j, PLANE)

    barrier = pltpu.get_barrier_semaphore()
    others = [above, below] + [peer(j) for j in range(1, PLANE)]
    for other in others:
        pl.semaphore_signal(barrier, inc=1, device_id={"clu": other}, device_id_type=MESH)
    pl.semaphore_wait(barrier, len(others))

    def ring(d, s, up):
        held = ups if up else downs
        target = last if d == half else held[d]
        rows = pl.ds(s * step, step)
        index = d if up or d == half else planes - d
        return pltpu.make_async_remote_copy(
            src_ref=held[d - 1].at[rows],
            dst_ref=target.at[rows],
            send_sem=(up_send if up else down_send).at[d - 1, s],
            recv_sem=ring_recv.at[index, s],
            device_id={"clu": above if up else below},
            device_id_type=MESH,
        )

    def travels(d, s, up):
        return d < half or (d == half and (s < SUBS // 2) == up)

    def side(k, j, source_slot):
        return pltpu.make_async_remote_copy(
            src_ref=stage.at[k * (PLANE - 1) + j - 1],
            dst_ref=out_ref.at[k * PLANE + source_slot],
            send_sem=side_send.at[k, j - 1],
            recv_sem=side_recv.at[k, source_slot],
            device_id={"clu": peer(j)},
            device_id_type=MESH,
        )

    def spread(k, held):
        out_ref[k * PLANE + i] = held[pick_ref[k * PLANE]]
        for j in range(1, PLANE):
            stage[k * (PLANE - 1) + j - 1] = held[pick_ref[k * PLANE + j]]
            side(k, j, i).start()

    for s in range(SUBS):
        ring(1, s, True).start()
        ring(1, s, False).start()
    spread(0, kv_ref)
    for d in range(1, half + 1):
        for s in range(SUBS):
            for up in (True, False):
                if travels(d, s, up):
                    ring(d, s, up).wait_recv()
                    if travels(d + 1, s, up):
                        ring(d + 1, s, up).start()
        if d < half:
            spread(d, ups[d])
            spread(planes - d, downs[d])
        else:
            spread(d, last)

    for d in range(1, half + 1):
        for s in range(SUBS):
            for up in (True, False):
                if travels(d, s, up):
                    ring(d, s, up).wait_send()

    def finish(k, carry):
        for j in range(1, PLANE):
            side(k, j, i).wait_send()
            side(k, j, lax.rem(i + PLANE - j, PLANE)).wait_recv()
        return carry

    lax.fori_loop(0, planes, finish, 0)


def ring_fetch(picks, kv, groups):
    planes = groups // PLANE
    block = kv.shape[1:]
    return pl.pallas_call(
        functools.partial(ring_kernel, planes),
        out_shape=jax.ShapeDtypeStruct((groups,) + block, kv.dtype),
        in_specs=[
            pl.BlockSpec(memory_space=pltpu.SMEM),
            pl.BlockSpec(memory_space=pltpu.VMEM),
        ],
        out_specs=pl.BlockSpec(memory_space=pltpu.VMEM),
        scratch_shapes=[pltpu.VMEM(kv.shape, kv.dtype)] * (planes - 1)
        + [
            pltpu.VMEM((planes * (PLANE - 1),) + block, kv.dtype),
            pltpu.SemaphoreType.DMA((planes // 2, SUBS)),
            pltpu.SemaphoreType.DMA((planes // 2, SUBS)),
            pltpu.SemaphoreType.DMA((planes, SUBS)),
            pltpu.SemaphoreType.DMA((planes, PLANE - 1)),
            pltpu.SemaphoreType.DMA((planes, PLANE)),
        ],
        compiler_params=pltpu.CompilerParams(
            collective_id=0, has_side_effects=True, vmem_limit_bytes=44 * 2**20
        ),
        cost_estimate=pl.CostEstimate(flops=0, bytes_accessed=2**25, transcendentals=0),
        name="ring_fetch",
    )(picks, kv)


def attend_kernel(listed, loc_ref, q_ref, kv_ref, far_ref, o_ref):
    features = q_ref.shape[2]
    heads = features // HD
    keys = (1 + listed) * CSIZE
    scale = 1.0 / math.sqrt(HD)
    row_cluster = lax.broadcasted_iota(jnp.int32, (2 * CSIZE, 2 * keys), 0) // CSIZE
    key_cluster = lax.broadcasted_iota(jnp.int32, (2 * CSIZE, 2 * keys), 1) // keys
    own = row_cluster == key_cluster

    def body(pair, carry):
        tiles = []
        for c in (2 * pair, 2 * pair + 1):
            tiles.append((kv_ref, c))
            for p in range(listed):
                tiles.append((far_ref, loc_ref[c * listed + p]))
        for h in range(heads):
            q = jnp.concatenate([q_ref[2 * pair + n, :, h * HD : (h + 1) * HD] for n in range(2)], axis=0)
            k = jnp.concatenate([ref[at, :, h * HD : (h + 1) * HD] for ref, at in tiles], axis=0)
            v = jnp.concatenate(
                [ref[at, :, features + h * HD : features + (h + 1) * HD] for ref, at in tiles], axis=0
            )
            scores = lax.dot_general(q, k, (((1,), (1,)), ((), ())), preferred_element_type=F32) * scale
            scores = jnp.where(own, scores, -jnp.inf)
            powers = jnp.exp(scores - jnp.max(scores, axis=-1, keepdims=True))
            weights = (powers / jnp.sum(powers, axis=-1, keepdims=True)).astype(BF16)
            result = jnp.dot(weights, v, preferred_element_type=F32).astype(BF16)
            for n in range(2):
                o_ref[2 * pair + n, :, h * HD : (h + 1) * HD] = result[n * CSIZE : (n + 1) * CSIZE]
        return carry

    lax.fori_loop(0, q_ref.shape[0] // 2, body, 0)


def attend(loc, q, kv, far, listed):
    return pl.pallas_call(
        functools.partial(attend_kernel, listed),
        out_shape=jax.ShapeDtypeStruct(q.shape, q.dtype),
        in_specs=[
            pl.BlockSpec(memory_space=pltpu.SMEM),
            pl.BlockSpec(memory_space=pltpu.VMEM),
            pl.BlockSpec(memory_space=pltpu.VMEM),
            pl.BlockSpec(memory_space=pltpu.VMEM),
        ],
        out_specs=pl.BlockSpec(memory_space=pltpu.VMEM),
        compiler_params=pltpu.CompilerParams(vmem_limit_bytes=32 * 2**20),
        cost_estimate=pl.CostEstimate(flops=2**27, bytes_accessed=2**23, transcendentals=2**19),
        name="attend",
    )(loc, q, kv, far)


def onehot(index, count):
    return (jnp.arange(count, dtype=jnp.int32)[:, None] == index[None, :]).astype(BF16)


def exact(a, b):
    return jnp.dot(a, b, preferred_element_type=F32)


def shards(query, key, value, labels, partners, out_weight):
    groups = lax.axis_size("clu")
    device = lax.axis_index("clu")
    tokens, features = query.shape
    per_device = tokens // CSIZE
    listed = partners.shape[1]
    quota = (3 * tokens + 2 * groups - 1) // (2 * groups)
    slots = groups * quota
    planes = groups // PLANE
    z, i = device // PLANE, device % PLANE

    owner = labels // per_device
    before = jnp.arange(tokens)[None, :] < jnp.arange(tokens)[:, None]
    rank = jnp.sum((owner[:, None] == owner[None, :]) & before, axis=1, dtype=jnp.int32)
    slot = owner * quota + rank
    packer = onehot(slot, slots)
    rows = jnp.concatenate([key, value, query], axis=1)
    packed = exact(packer, rows).astype(BF16).reshape(groups, quota, 3 * features)
    arrived = lax.all_to_all(packed, "clu", split_axis=0, concat_axis=0, tiled=True)
    arrived = arrived.reshape(slots, 3 * features)

    all_labels = lax.all_gather(labels, "clu").reshape(groups, tokens)
    mine = all_labels // per_device == device
    upto = (jnp.arange(tokens)[:, None] <= jnp.arange(tokens)[None, :]).astype(BF16)
    order = exact(mine.astype(BF16), upto).astype(jnp.int32) - 1
    local = jnp.where(mine, all_labels - device * per_device + 1, 0)
    tags = jnp.stack(
        [jnp.sum(jnp.where(order == r, local, 0), axis=1) for r in range(quota)], axis=1
    ).reshape(slots) - 1
    earlier = jnp.arange(slots)[None, :] < jnp.arange(slots)[:, None]
    position = jnp.sum((tags[:, None] == tags[None, :]) & earlier, axis=1, dtype=jnp.int32)
    destination = jnp.where(tags >= 0, tags * CSIZE + position, -1)
    placer = onehot(destination, tokens)
    placed = exact(placer, arrived).astype(BF16)
    kv = placed[:, : 2 * features].reshape(per_device, CSIZE, 2 * features)
    queries = placed[:, 2 * features :].reshape(per_device, CSIZE, features)

    wanted = partners.reshape(groups, per_device * listed)
    plane = lax.dynamic_slice_in_dim(wanted, z * PLANE, PLANE, 0)
    plane = jnp.take(plane, (i + jnp.arange(PLANE)) % PLANE, axis=0)
    source = (z - jnp.arange(planes)) % planes * PLANE + i
    hit = plane[None] // per_device == source[:, None, None]
    picks = jnp.sum(jnp.where(hit, plane[None] - source[:, None, None] * per_device, 0), axis=2)
    my_list = lax.dynamic_slice_in_dim(wanted, device, 1, 0)[0]
    from_group = my_list // per_device
    location = (z - from_group // PLANE) % planes * PLANE + from_group % PLANE

    far = ring_fetch(picks.reshape(-1).astype(jnp.int32), kv, groups)
    attended = attend(location.astype(jnp.int32), queries, kv, far, listed).reshape(tokens, features)

    outgoing = exact(placer.T, attended).astype(BF16).reshape(groups, quota, features)
    returned = lax.all_to_all(outgoing, "clu", split_axis=0, concat_axis=0, tiled=True)
    token_rows = exact(packer.T, returned.reshape(slots, features)).astype(BF16)
    partial_value = exact(token_rows, lax.all_gather(out_weight, "clu", axis=1, tiled=True))
    return lax.psum_scatter(partial_value.astype(BF16), "head", scatter_dimension=1, tiled=True)


def solution(mesh):
    return jax.shard_map(
        shards,
        mesh=mesh,
        in_specs=(
            P("clu", "head"),
            P("clu", "head"),
            P("clu", "head"),
            P("clu"),
            P(),
            P("head", "clu"),
        ),
        out_specs=P("clu", "head"),
        check_vma=False,
    )
```

```python
import functools
import math

import jax
import jax.numpy as jnp
from jax import lax
from jax.experimental import pallas as pl
from jax.experimental.pallas import tpu as pltpu
from jax.sharding import PartitionSpec as P

HD = 128
CSIZE = 16
PLANE = 8
SUBS = 4
MESH = pl.DeviceIdType.MESH
F32 = jnp.float32
BF16 = jnp.bfloat16


def ring_kernel(planes, pick_ref, kv_ref, out_ref, *rest):
    half = planes // 2
    ups = (kv_ref,) + rest[: half - 1]
    downs = (kv_ref,) + rest[half - 1 : 2 * half - 2]
    last = rest[2 * half - 2]
    stage, up_send, down_send, ring_recv, side_send, side_recv = rest[2 * half - 1 :]
    me = lax.axis_index("clu")
    z, i = me // PLANE, me % PLANE
    above = lax.rem(z + 1, planes) * PLANE + i
    below = lax.rem(z + planes - 1, planes) * PLANE + i
    step = kv_ref.shape[0] // SUBS

    def peer(j):
        return z * PLANE + lax.rem(i + j, PLANE)

    barrier = pltpu.get_barrier_semaphore()
    others = [above, below] + [peer(j) for j in range(1, PLANE)]
    for other in others:
        pl.semaphore_signal(barrier, inc=1, device_id={"clu": other}, device_id_type=MESH)
    pl.semaphore_wait(barrier, len(others))

    def ring(d, s, up):
        held = ups if up else downs
        target = last if d == half else held[d]
        rows = pl.ds(s * step, step)
        index = d if up or d == half else planes - d
        return pltpu.make_async_remote_copy(
            src_ref=held[d - 1].at[rows],
            dst_ref=target.at[rows],
            send_sem=(up_send if up else down_send).at[d - 1, s],
            recv_sem=ring_recv.at[index, s],
            device_id={"clu": above if up else below},
            device_id_type=MESH,
        )

    def travels(d, s, up):
        return d < half or (d == half and (s < SUBS // 2) == up)

    def side(k, j, source_slot):
        return pltpu.make_async_remote_copy(
            src_ref=stage.at[k * (PLANE - 1) + j - 1],
            dst_ref=out_ref.at[k * PLANE + source_slot],
            send_sem=side_send.at[k, j - 1],
            recv_sem=side_recv.at[k, source_slot],
            device_id={"clu": peer(j)},
            device_id_type=MESH,
        )

    def spread(k, held):
        out_ref[k * PLANE + i] = held[pick_ref[k * PLANE]]
        for j in range(1, PLANE):
            stage[k * (PLANE - 1) + j - 1] = held[pick_ref[k * PLANE + j]]
            side(k, j, i).start()

    for s in range(SUBS):
        ring(1, s, True).start()
        ring(1, s, False).start()
    spread(0, kv_ref)
    for d in range(1, half + 1):
        for s in range(SUBS):
            for up in (True, False):
                if travels(d, s, up):
                    ring(d, s, up).wait_recv()
                    if travels(d + 1, s, up):
                        ring(d + 1, s, up).start()
        if d < half:
            spread(d, ups[d])
            spread(planes - d, downs[d])
        else:
            spread(d, last)

    for d in range(1, half + 1):
        for s in range(SUBS):
            for up in (True, False):
                if travels(d, s, up):
                    ring(d, s, up).wait_send()

    def finish(k, carry):
        for j in range(1, PLANE):
            side(k, j, i).wait_send()
            side(k, j, lax.rem(i + PLANE - j, PLANE)).wait_recv()
        return carry

    lax.fori_loop(0, planes, finish, 0)


def ring_fetch(picks, kv, groups):
    planes = groups // PLANE
    block = kv.shape[1:]
    return pl.pallas_call(
        functools.partial(ring_kernel, planes),
        out_shape=jax.ShapeDtypeStruct((groups,) + block, kv.dtype),
        in_specs=[
            pl.BlockSpec(memory_space=pltpu.SMEM),
            pl.BlockSpec(memory_space=pltpu.VMEM),
        ],
        out_specs=pl.BlockSpec(memory_space=pltpu.VMEM),
        scratch_shapes=[pltpu.VMEM(kv.shape, kv.dtype)] * (planes - 1)
        + [
            pltpu.VMEM((planes * (PLANE - 1),) + block, kv.dtype),
            pltpu.SemaphoreType.DMA((planes // 2, SUBS)),
            pltpu.SemaphoreType.DMA((planes // 2, SUBS)),
            pltpu.SemaphoreType.DMA((planes, SUBS)),
            pltpu.SemaphoreType.DMA((planes, PLANE - 1)),
            pltpu.SemaphoreType.DMA((planes, PLANE)),
        ],
        compiler_params=pltpu.CompilerParams(
            collective_id=0, has_side_effects=True, vmem_limit_bytes=44 * 2**20
        ),
        cost_estimate=pl.CostEstimate(flops=0, bytes_accessed=2**25, transcendentals=0),
        name="ring_fetch",
    )(picks, kv)


def exchange_kernel(planes, labels_ref, block_ref, out_ref, all_ref, send, recv, tag_send, tag_recv, side_send, side_recv, own):
    me = lax.axis_index("clu")
    z, i = me // PLANE, me % PLANE
    half = planes // 2
    hops = [half]
    for d in range(half - 1, 0, -1):
        hops += [-d, d]

    def at(dz, j):
        return lax.rem(z + dz + planes, planes) * PLANE + lax.rem(i + j + PLANE, PLANE)

    barrier = pltpu.get_barrier_semaphore()

    def greet(r, carry):
        other = lax.rem(me + r, planes * PLANE)
        pl.semaphore_signal(barrier, inc=1, device_id={"clu": other}, device_id_type=MESH)
        return carry

    lax.fori_loop(1, planes * PLANE, greet, 0)
    pl.semaphore_wait(barrier, planes * PLANE - 1)

    def copy(to, source):
        return pltpu.make_async_remote_copy(
            src_ref=block_ref.at[to],
            dst_ref=out_ref.at[source],
            send_sem=send.at[to],
            recv_sem=recv.at[source],
            device_id={"clu": to},
            device_id_type=MESH,
        )

    def tag(dz, source):
        return pltpu.make_async_remote_copy(
            src_ref=labels_ref,
            dst_ref=all_ref.at[i, source],
            send_sem=tag_send.at[dz % planes],
            recv_sem=tag_recv.at[source],
            device_id={"clu": at(dz, 0)},
            device_id_type=MESH,
        )

    def side(j, source):
        return pltpu.make_async_remote_copy(
            src_ref=all_ref.at[i],
            dst_ref=all_ref.at[source],
            send_sem=side_send.at[j],
            recv_sem=side_recv.at[source],
            device_id={"clu": at(0, j)},
            device_id_type=MESH,
        )

    if labels_ref is not None:
        for dz in hops:
            tag(dz, z).start()

    def start(j, carry):
        for dz in hops:
            copy(at(dz, j), me).start()
        return carry

    def start_side(j, carry):
        copy(at(0, j), me).start()
        return carry

    lax.fori_loop(0, PLANE, start, 0)
    lax.fori_loop(1, PLANE, start_side, 0)
    mine = pltpu.make_async_copy(block_ref.at[me], out_ref.at[me], own.at[0])
    mine.start()
    if labels_ref is not None:
        mine_tags = pltpu.make_async_copy(labels_ref, all_ref.at[i, z], own.at[1])
        mine_tags.start()
        mine_tags.wait()
        for dz in hops:
            tag(dz, lax.rem(z - dz + planes, planes)).wait_recv()
        for j in range(1, PLANE):
            side(j, i).start()
        for j in range(1, PLANE):
            side(j, lax.rem(i - j + PLANE, PLANE)).wait_recv()
        for dz in hops:
            tag(dz, z).wait_send()
        for j in range(1, PLANE):
            side(j, i).wait_send()

    def finish(r, carry):
        copy(lax.rem(me + r, planes * PLANE), me).wait_send()
        copy(me, lax.rem(me + r, planes * PLANE)).wait_recv()
        return carry

    lax.fori_loop(1, planes * PLANE, finish, 0)
    mine.wait()


def deliver_kernel(planes, labels_ref, block_ref, out_ref, all_ref, *sems):
    exchange_kernel(planes, labels_ref, block_ref, out_ref, all_ref, *sems)


def give_back_kernel(planes, block_ref, out_ref, send, recv, own):
    exchange_kernel(planes, None, block_ref, out_ref, None, send, recv, None, None, None, None, own)


VMEM = pl.BlockSpec(memory_space=pltpu.VMEM)
SMEM = pl.BlockSpec(memory_space=pltpu.SMEM)


def deliver(labels, block):
    groups = block.shape[0]
    planes = groups // PLANE
    dma = pltpu.SemaphoreType.DMA
    return pl.pallas_call(
        functools.partial(deliver_kernel, planes),
        out_shape=(
            jax.ShapeDtypeStruct(block.shape, block.dtype),
            jax.ShapeDtypeStruct((PLANE, planes) + labels.shape, labels.dtype),
        ),
        in_specs=[VMEM, VMEM],
        out_specs=(VMEM, VMEM),
        scratch_shapes=[
            dma((groups,)), dma((groups,)), dma((planes,)), dma((planes,)), dma((PLANE,)), dma((PLANE,)), dma((2,)),
        ],
        compiler_params=pltpu.CompilerParams(
            collective_id=1, has_side_effects=True, vmem_limit_bytes=24 * 2**20
        ),
        cost_estimate=pl.CostEstimate(flops=0, bytes_accessed=2**25, transcendentals=0),
        name="deliver",
    )(labels, block)


def give_back(block):
    groups = block.shape[0]
    dma = pltpu.SemaphoreType.DMA
    return pl.pallas_call(
        functools.partial(give_back_kernel, groups // PLANE),
        out_shape=jax.ShapeDtypeStruct(block.shape, block.dtype),
        in_specs=[VMEM],
        out_specs=VMEM,
        scratch_shapes=[dma((groups,)), dma((groups,)), dma((1,))],
        compiler_params=pltpu.CompilerParams(
            collective_id=2, has_side_effects=True, vmem_limit_bytes=16 * 2**20
        ),
        cost_estimate=pl.CostEstimate(flops=0, bytes_accessed=2**24, transcendentals=0),
        name="give_back",
    )(block)


def attend_kernel(listed, loc_ref, q_ref, kv_ref, far_ref, o_ref):
    features = q_ref.shape[2]
    heads = features // HD
    keys = (1 + listed) * CSIZE
    scale = 1.0 / math.sqrt(HD)
    row_cluster = lax.broadcasted_iota(jnp.int32, (heads, 2 * CSIZE, 2 * keys), 1) // CSIZE
    key_cluster = lax.broadcasted_iota(jnp.int32, (heads, 2 * CSIZE, 2 * keys), 2) // keys
    own = row_cluster == key_cluster

    def body(pair, carry):
        tiles = []
        for c in (2 * pair, 2 * pair + 1):
            tiles.append((kv_ref, c))
            for p in range(listed):
                tiles.append((far_ref, loc_ref[c * listed + p]))
        scores, values = [], []
        for h in range(heads):
            q = jnp.concatenate([q_ref[2 * pair + n, :, h * HD : (h + 1) * HD] for n in range(2)], axis=0)
            k = jnp.concatenate([ref[at, :, h * HD : (h + 1) * HD] for ref, at in tiles], axis=0)
            scores.append(lax.dot_general(q, k, (((1,), (1,)), ((), ())), preferred_element_type=F32))
        scores = jnp.where(own, jnp.stack(scores) * scale, -jnp.inf)
        powers = jnp.exp(scores - jnp.max(scores, axis=-1, keepdims=True))
        weights = (powers / jnp.sum(powers, axis=-1, keepdims=True)).astype(BF16)
        for h in range(heads):
            v = jnp.concatenate(
                [ref[at, :, features + h * HD : features + (h + 1) * HD] for ref, at in tiles], axis=0
            )
            result = jnp.dot(weights[h], v, preferred_element_type=F32).astype(BF16)
            for n in range(2):
                o_ref[2 * pair + n, :, h * HD : (h + 1) * HD] = result[n * CSIZE : (n + 1) * CSIZE]
        return carry

    lax.fori_loop(0, q_ref.shape[0] // 2, body, 0)


def attend(loc, q, kv, far, listed):
    return pl.pallas_call(
        functools.partial(attend_kernel, listed),
        out_shape=jax.ShapeDtypeStruct(q.shape, q.dtype),
        in_specs=[
            pl.BlockSpec(memory_space=pltpu.SMEM),
            pl.BlockSpec(memory_space=pltpu.VMEM),
            pl.BlockSpec(memory_space=pltpu.VMEM),
            pl.BlockSpec(memory_space=pltpu.VMEM),
        ],
        out_specs=pl.BlockSpec(memory_space=pltpu.VMEM),
        compiler_params=pltpu.CompilerParams(vmem_limit_bytes=32 * 2**20),
        cost_estimate=pl.CostEstimate(flops=2**27, bytes_accessed=2**23, transcendentals=2**19),
        name="attend",
    )(loc, q, kv, far)


def onehot(index, count):
    return (jnp.arange(count, dtype=jnp.int32)[:, None] == index[None, :]).astype(BF16)


def exact(a, b):
    return jnp.dot(a, b, preferred_element_type=F32)


def shards(query, key, value, labels, partners, out_weight):
    groups = lax.axis_size("clu")
    device = lax.axis_index("clu")
    tokens, features = query.shape
    per_device = tokens // CSIZE
    listed = partners.shape[1]
    quota = (3 * tokens + 2 * groups - 1) // (2 * groups)
    slots = groups * quota
    planes = groups // PLANE
    z, i = device // PLANE, device % PLANE

    owner = labels // per_device
    before = jnp.arange(tokens)[None, :] < jnp.arange(tokens)[:, None]
    rank = jnp.sum((owner[:, None] == owner[None, :]) & before, axis=1, dtype=jnp.int32)
    slot = owner * (2 * quota) + rank
    packer = onehot(jnp.concatenate([slot, slot + quota]), 2 * slots)
    wide = 3 * features // 2
    rows = jnp.concatenate(
        [
            jnp.concatenate([key, value[:, : wide - features]], axis=1),
            jnp.concatenate([value[:, wide - features :], query], axis=1),
        ],
        axis=0,
    )
    packed = exact(packer, rows).astype(BF16).reshape(groups, 2 * quota, wide)
    arrived, all_labels = deliver(labels.reshape(1, tokens), packed)
    arrived = arrived.reshape(2 * slots, wide)

    all_labels = all_labels.reshape(PLANE, planes, tokens).transpose(1, 0, 2).reshape(groups, tokens)
    mine = all_labels // per_device == device
    upto = (jnp.arange(tokens)[:, None] <= jnp.arange(tokens)[None, :]).astype(BF16)
    order = exact(mine.astype(BF16), upto).astype(jnp.int32) - 1
    local = jnp.where(mine, all_labels - device * per_device + 1, 0)
    tags = jnp.stack(
        [jnp.sum(jnp.where(order == r, local, 0), axis=1) for r in range(quota)], axis=1
    ).reshape(slots) - 1
    earlier = jnp.arange(slots)[None, :] < jnp.arange(slots)[:, None]
    position = jnp.sum((tags[:, None] == tags[None, :]) & earlier, axis=1, dtype=jnp.int32)
    destination = jnp.where(tags >= 0, tags * CSIZE + position, -1).reshape(groups, quota)
    nowhere = jnp.full_like(destination, -1)
    placer = jnp.concatenate(
        [
            onehot(jnp.concatenate([destination, nowhere], axis=1).reshape(-1), tokens),
            onehot(jnp.concatenate([nowhere, destination], axis=1).reshape(-1), tokens),
        ],
        axis=0,
    )
    placed = exact(placer, arrived).astype(BF16)
    kv = jnp.concatenate([placed[:tokens], placed[tokens:, : 2 * features - wide]], axis=1)
    kv = kv.reshape(per_device, CSIZE, 2 * features)
    queries = placed[tokens:, 2 * features - wide :].reshape(per_device, CSIZE, features)

    wanted = partners.reshape(groups, per_device * listed)
    plane = lax.dynamic_slice_in_dim(wanted, z * PLANE, PLANE, 0)
    plane = jnp.take(plane, (i + jnp.arange(PLANE)) % PLANE, axis=0)
    source = (z - jnp.arange(planes)) % planes * PLANE + i
    hit = plane[None] // per_device == source[:, None, None]
    picks = jnp.sum(jnp.where(hit, plane[None] - source[:, None, None] * per_device, 0), axis=2)
    my_list = lax.dynamic_slice_in_dim(wanted, device, 1, 0)[0]
    from_group = my_list // per_device
    location = (z - from_group // PLANE) % planes * PLANE + from_group % PLANE

    far = ring_fetch(picks.reshape(-1).astype(jnp.int32), kv, groups)
    attended = attend(location.astype(jnp.int32), queries, kv, far, listed).reshape(tokens, features)

    halves = jnp.concatenate([attended[:, : features // 2], attended[:, features // 2 :]], axis=0)
    outgoing = exact(placer.T, halves).astype(BF16).reshape(groups, 2 * quota, features // 2)
    returned = give_back(outgoing).reshape(2 * slots, features // 2)
    token_rows = exact(packer.T, returned).astype(BF16)
    token_rows = jnp.concatenate([token_rows[:tokens], token_rows[tokens:]], axis=1)
    partial_value = exact(token_rows, lax.all_gather(out_weight, "clu", axis=1, tiled=True))
    return lax.psum_scatter(partial_value.astype(BF16), "head", scatter_dimension=1, tiled=True)


def solution(mesh):
    return jax.shard_map(
        shards,
        mesh=mesh,
        in_specs=(
            P("clu", "head"),
            P("clu", "head"),
            P("clu", "head"),
            P("clu"),
            P(),
            P("head", "clu"),
        ),
        out_specs=P("clu", "head"),
        check_vma=False,
    )
```

```python
import functools
import math

import jax
import jax.numpy as jnp
import numpy as np
from jax import lax
from jax.experimental import pallas as pl
from jax.experimental.pallas import tpu as pltpu
from jax.sharding import PartitionSpec as P

HD = 128
CSIZE = 16
PLANE = 8
SUBS = 4
GROUPS = (4, 2)
LANES = 128
MESH = pl.DeviceIdType.MESH
F32 = jnp.float32
BF16 = jnp.bfloat16
VMEM = pl.BlockSpec(memory_space=pltpu.VMEM)
SMEM = pl.BlockSpec(memory_space=pltpu.SMEM)


def drain(ref, count, sem):
    some = ref.at[pl.ds(0, count)]
    pltpu.make_async_copy(some, some, sem).wait()


def exact(a, b):
    return jnp.dot(a, b, preferred_element_type=F32)


class Ring:
    def __init__(self, planes, z, i, pick, kv, out, ups, downs, packs, near, far, stage, sems):
        self.planes, self.half, self.full = planes, planes // 2, planes // 2 - 2
        self.z, self.i = z, i
        self.above = lax.rem(z + 1, planes) * PLANE + i
        self.below = lax.rem(z + planes - 1, planes) * PLANE + i
        self.pick, self.kv, self.out = pick, kv, out
        self.ups, self.downs = (kv,) + ups, (kv,) + downs
        self.packs, self.near, self.far, self.stage = packs, near, far, stage
        self.ring_send, self.ring_recv, self.pack_send, self.pack_recv, self.side_send, self.side_recv = sems
        self.step = kv.shape[0] // SUBS
        self.part = PLANE // 2

    def send_on(self, src, dst, send, recv, up):
        return pltpu.make_async_remote_copy(
            src_ref=src,
            dst_ref=dst,
            send_sem=send,
            recv_sem=recv,
            device_id={"clu": self.above if up else self.below},
            device_id_type=MESH,
        )

    def hop(self, d, s, up):
        held = self.ups if up else self.downs
        rows = pl.ds(s * self.step, self.step)
        n = 0 if up else 1
        return self.send_on(
            held[d - 1].at[rows], held[d].at[rows], self.ring_send.at[n, d - 1, s], self.ring_recv.at[n, d - 1, s], up
        )

    def pack(self, at, up):
        n = 0 if up else 1
        rows = pl.ds(0, self.part) if at == 0 else pl.ds(self.part, PLANE)
        return self.send_on(
            self.packs.at[n, rows], self.near.at[n, rows], self.pack_send.at[n, at], self.pack_recv.at[n, at], up
        )

    def pack_on(self, up):
        n = 0 if up else 1
        return self.send_on(
            self.near.at[n, pl.ds(0, self.part)], self.far.at[n], self.pack_send.at[n, 2], self.pack_recv.at[n, 2], up
        )

    def side(self, k, j, src):
        return pltpu.make_async_remote_copy(
            src_ref=src,
            dst_ref=self.out.at[k * PLANE + self.i],
            send_sem=self.side_send,
            recv_sem=self.side_recv,
            device_id={"clu": self.z * PLANE + lax.rem(self.i + j, PLANE)},
            device_id_type=MESH,
        )

    def spread(self, k, held):
        self.out[k * PLANE + self.i] = held[self.pick[k * PLANE]]
        for j in range(1, PLANE):
            at = k * (PLANE - 1) + j - 1
            self.stage[at] = held[self.pick[k * PLANE + j]]
            self.side(k, j, self.stage.at[at]).start()

    def pass_out(self, k, j, src):
        if j == 0:
            self.out[k * PLANE + self.i] = src[...]
        else:
            self.side(k, j, src).start()

    def begin(self):
        for s in range(SUBS):
            for up in (True, False):
                self.hop(1, s, up).start()
        self.spread(0, self.kv)

    def advance(self, d):
        for s in range(SUBS):
            for up in (True, False):
                self.hop(d, s, up).wait_recv()
                if d < self.full:
                    self.hop(d + 1, s, up).start()
        if d == self.full:
            for up in (True, False):
                n = 0 if up else 1
                held = (self.ups if up else self.downs)[d]
                base = (self.planes + 2 * n) * PLANE
                for j in range(self.part):
                    self.packs[n, j] = held[self.pick[base + n * self.part + j]]
                self.pack(0, up).start()
                for j in range(PLANE):
                    self.packs[n, self.part + j] = held[self.pick[base + PLANE + j]]
                self.pack(1, up).start()
        self.spread(d, self.ups[d])
        self.spread(self.planes - d, self.downs[d])

    def last_hops(self):
        for up in (True, False):
            self.pack(0, up).wait_recv()
            self.pack_on(up).start()
        for up in (True, False):
            n = 0 if up else 1
            self.pack(1, up).wait_recv()
            for j in range(PLANE):
                self.pass_out(self.full + 1 if up else self.planes - self.full - 1, j, self.near.at[n, self.part + j])
        for up in (True, False):
            n = 0 if up else 1
            self.pack_on(up).wait_recv()
            for j in range(self.part):
                self.pass_out(self.half, n * self.part + j, self.far.at[n, j])

    def arrive(self):
        drain(self.out, self.planes * (PLANE - 1), self.side_recv)

    def finish(self):
        for up in (True, False):
            for d in range(1, self.full + 1):
                for s in range(SUBS):
                    self.hop(d, s, up).wait_send()
            self.pack(0, up).wait_send()
            self.pack(1, up).wait_send()
            self.pack_on(up).wait_send()
        drain(self.stage, self.planes * (PLANE - 1), self.side_send)


def attend(listed, first, heads, loc_ref, q_ref, kv_ref, far_ref, o_ref):
    keys = (1 + listed) * CSIZE
    width = heads * HD
    scale = 1.0 / math.sqrt(HD)
    shape = (heads, 2 * CSIZE, 2 * keys)
    row, key = lax.broadcasted_iota(jnp.int32, shape, 1), lax.broadcasted_iota(jnp.int32, shape, 2)
    own = (row >= CSIZE) == (key >= keys)

    def body(pair, carry):
        tiles = []
        for c in (2 * pair, 2 * pair + 1):
            tiles.append((kv_ref, c))
            for p in range(listed):
                tiles.append((far_ref, loc_ref[c * listed + p]))
        scores = []
        for h in range(heads):
            at = (first + h) * HD
            q = jnp.concatenate([q_ref[2 * pair + n, :, at : at + HD] for n in range(2)], axis=0)
            k = jnp.concatenate([ref[at, :, h * HD : (h + 1) * HD] for ref, at in tiles], axis=0)
            scores.append(lax.dot_general(q, k, (((1,), (1,)), ((), ())), preferred_element_type=F32))
        scores = jnp.where(own, jnp.stack(scores) * scale, -jnp.inf)
        powers = jnp.exp(scores - jnp.max(scores, axis=-1, keepdims=True))
        weights = (powers / jnp.sum(powers, axis=-1, keepdims=True)).astype(BF16)
        for h in range(heads):
            v = jnp.concatenate([ref[at, :, width + h * HD : width + (h + 1) * HD] for ref, at in tiles], axis=0)
            o_ref[pl.ds(2 * CSIZE * pair, 2 * CSIZE), h * HD : (h + 1) * HD] = exact(weights[h], v).astype(BF16)
        return carry

    lax.fori_loop(0, q_ref.shape[0] // 2, body, 0)


def layer_kernel(planes, listed, *refs):
    (pick, loc, labels_ref, send0, send1, sendq, upto, lower, col, row, col_mask, row_mask, ret0, ret1, *rest) = refs
    (arr0, arr1, arrq, all_ref, lab, dcol, drow, q_ref, back0, back1, o0, o1, *rest) = rest
    (a2a_send, a2a_recv, tag_send, tag_recv, tag_side_send, tag_side_recv, *rest) = rest
    per_ring = len(rest) // 2
    me = lax.axis_index("clu")
    z, i = me // PLANE, me % PLANE
    half, full, total = planes // 2, planes // 2 - 2, planes * PLANE
    hops = [half]
    for d in range(half - 1, 0, -1):
        hops += [-d, d]

    rings = []
    for g in range(2):
        kv, out, *more = rest[g * per_ring : (g + 1) * per_ring]
        ups, downs, more = tuple(more[:full]), tuple(more[full : 2 * full]), more[2 * full :]
        rings.append(Ring(planes, z, i, pick, kv, out, ups, downs, *more[:4], more[4:]))

    def at(dz, j):
        return lax.rem(z + dz + planes, planes) * PLANE + lax.rem(i + j, PLANE)

    barrier = pltpu.get_barrier_semaphore()

    def greet(r, carry):
        other = lax.rem(me + r, total)
        pl.semaphore_signal(barrier, inc=1, device_id={"clu": other}, device_id_type=MESH)
        return carry

    lax.fori_loop(1, total, greet, 0)
    pl.semaphore_wait(barrier, total - 1)

    def tag(dz, source):
        return pltpu.make_async_remote_copy(
            src_ref=labels_ref,
            dst_ref=all_ref.at[i, source],
            send_sem=tag_send.at[dz % planes],
            recv_sem=tag_recv.at[source],
            device_id={"clu": at(dz, 0)},
            device_id_type=MESH,
        )

    def tag_side(j, source):
        return pltpu.make_async_remote_copy(
            src_ref=all_ref.at[i],
            dst_ref=all_ref.at[source],
            send_sem=tag_side_send.at[j],
            recv_sem=tag_side_recv.at[source],
            device_id={"clu": at(0, j)},
            device_id_type=MESH,
        )

    def exchange(n, block, landed):
        def start(to):
            pltpu.make_async_remote_copy(
                src_ref=block.at[to],
                dst_ref=landed.at[me],
                send_sem=a2a_send.at[n],
                recv_sem=a2a_recv.at[n],
                device_id={"clu": to},
                device_id_type=MESH,
            ).start()

        def far(j, carry):
            for dz in hops:
                start(at(dz, j))
            return carry

        def close(j, carry):
            start(at(0, j))
            return carry

        lax.fori_loop(0, PLANE, far, 0)
        lax.fori_loop(1, PLANE, close, 0)
        landed[me] = block[me]

    def landed_all(n, landed):
        drain(landed, total - 1, a2a_recv.at[n])

    for dz in hops:
        tag(dz, z).start()
    all_ref[i, z] = labels_ref[...]
    exchange(0, send0, arr0)
    for dz in hops:
        tag(dz, lax.rem(z - dz + planes, planes)).wait_recv()
    for j in range(1, PLANE):
        tag_side(j, i).start()
    exchange(1, send1, arr1)
    exchange(2, sendq, arrq)
    for j in range(1, PLANE):
        tag_side(j, lax.rem(i - j + PLANE, PLANE)).wait_recv()

    for zz in range(planes):
        for ii in range(PLANE):
            lab[zz * PLANE + ii : zz * PLANE + ii + 1, :] = all_ref[ii, zz]
    per_device = q_ref.shape[0]
    quota = send0.shape[1] // 2
    local = lab[...] - me * per_device
    mine = jnp.logical_and(local >= 0, local < per_device)
    order = exact(jnp.where(mine, 1.0, 0.0).astype(BF16), upto[...])
    named = jnp.where(mine, (local + 1).astype(F32), 0.0)
    lane = lax.broadcasted_iota(jnp.int32, (total, LANES), 1)
    lanef = lane.astype(F32)
    tags, marks = [], []
    for r in range(quota):
        one = jnp.sum(jnp.where(order == r + 1.0, named, 0.0), axis=1, keepdims=True)
        one = jnp.where(one > 0.0, one - 1.0, -100.0)
        tags.append(one)
        marks.append(jnp.where(lanef == one, 1.0, 0.0))
    earlier = exact(lower[...], sum(marks).astype(BF16))
    table = jnp.where(lane == 2 * quota, 1.0, 0.0)
    for r in range(quota):
        place = jnp.sum(marks[r] * earlier, axis=1, keepdims=True)
        table = jnp.where(lane == r, tags[r], jnp.where(lane == quota + r, place, table))
        earlier = earlier + marks[r]
    wide = exact(col[...], table.astype(BF16))
    tall = exact(table.T.astype(BF16), row[...])
    slots, tokens = dcol.shape[1], dcol.shape[2]
    for p in range(2):
        to = jnp.sum(wide * col_mask[p], axis=1, keepdims=True)
        rows = lax.broadcasted_iota(jnp.int32, (slots, tokens), 1).astype(F32)
        dcol[p] = jnp.where(rows == to, 1.0, 0.0).astype(BF16)
        to = jnp.sum(tall * row_mask[p], axis=0, keepdims=True)
        rows = lax.broadcasted_iota(jnp.int32, (tokens, slots), 0).astype(F32)
        drow[p] = jnp.where(rows == to, 1.0, 0.0).astype(BF16)

    def unpack(landed, target):
        width = landed.shape[2]
        for l in range(0, width, LANES):
            block = landed[:, :, l : l + LANES].astype(F32).reshape(slots, LANES).astype(BF16)
            for p in range(2):
                part = exact(drow[p], block).astype(BF16).reshape(per_device, CSIZE, LANES)
                target[:, :, p * width + l : p * width + l + LANES] = part

    def give_back(n, attended, back, ret):
        width = back.shape[2]
        for l in range(0, width, LANES):
            part = exact(dcol[0], attended[:, l : l + LANES]) + exact(dcol[1], attended[:, width + l : width + l + LANES])
            back[:, :, l : l + LANES] = part.reshape(total, 2 * quota, LANES).astype(BF16)
        exchange(n, back, ret)

    first, second = rings
    landed_all(0, arr0)
    unpack(arr0, first.kv)
    first.begin()
    for d in range(1, full + 1):
        first.advance(d)
    landed_all(1, arr1)
    unpack(arr1, second.kv)
    second.begin()
    first.last_hops()
    landed_all(2, arrq)
    unpack(arrq, q_ref)
    second.advance(1)
    first.arrive()
    attend(listed, 0, GROUPS[0], loc, q_ref, first.kv, first.out, o0)
    second.advance(2)
    give_back(3, o0, back0, ret0)
    for d in range(3, full + 1):
        second.advance(d)
    second.last_hops()
    second.arrive()
    attend(listed, GROUPS[0], GROUPS[1], loc, q_ref, second.kv, second.out, o1)
    give_back(4, o1, back1, ret1)

    for dz in hops:
        tag(dz, z).wait_send()
    for j in range(1, PLANE):
        tag_side(j, i).wait_send()
    first.finish()
    second.finish()
    for n, block in enumerate((send0, send1, sendq, back0, back1)):
        drain(block, total - 1, a2a_send.at[n])
    landed_all(3, ret0)
    landed_all(4, ret1)


def project_kernel(rows_ref, weight_ref, out_ref, sent, came, near, send, recv):
    n = lax.axis_size("head")
    x = lax.axis_index("head")
    left, right = lax.rem(x + n - 1, n), lax.rem(x + 1, n)
    width = out_ref.shape[1]
    part = width // 2

    def block(to, first, count):
        start = pl.multiple_of(to * width + first, LANES)
        return exact(rows_ref[...], weight_ref[:, pl.ds(start, count)])

    barrier = pltpu.get_barrier_semaphore()
    for other in (left, right):
        pl.semaphore_signal(barrier, inc=1, device_id={"head": other}, device_id_type=MESH)

    def copy(way, piece, src, dst):
        return pltpu.make_async_remote_copy(
            src_ref=src,
            dst_ref=dst,
            send_sem=send.at[way, piece],
            recv_sem=recv.at[way, piece],
            device_id={"head": right if way == 0 else left},
            device_id_type=MESH,
        )

    copies = [[copy(w, 0, sent.at[w, 0], near.at[w])] + [copy(w, p, sent.at[w, p], came.at[w, p - 1]) for p in (1, 2)] for w in range(2)]
    opposite = lax.rem(x + 2, n)
    for w in range(2):
        sent[w, 0] = block(opposite, w * part, part).astype(BF16)
    pl.semaphore_wait(barrier, 2)
    for w in range(2):
        copies[w][0].start()
    for w in range(2):
        sent[w, 1] = block(right if w == 0 else left, (1 - w) * part, part).astype(BF16)
        copies[w][1].start()
    summed = [block(right if w == 0 else left, w * part, part) for w in range(2)]
    for w in range(2):
        copies[w][0].wait_recv()
        sent[w, 2] = (summed[w].astype(BF16).astype(F32) + near[w].astype(F32)).astype(BF16)
        copies[w][2].start()
    own = [block(x, h * part, part).astype(BF16).astype(F32) for h in range(2)]
    for w in range(2):
        copies[w][1].wait_recv()
    for w in range(2):
        copies[w][2].wait_recv()
    for h in range(2):
        total = own[h]
        for w in range(2):
            total = total + came[w, 1 if h == w else 0].astype(F32)
        out_ref[:, h * part : (h + 1) * part] = total.astype(BF16)
    for w in range(2):
        for p in range(3):
            copies[w][p].wait_send()


def project(rows, weight, width):
    tokens = rows.shape[0]
    half = (tokens, width // 2)
    dma = pltpu.SemaphoreType.DMA
    return pl.pallas_call(
        project_kernel,
        out_shape=jax.ShapeDtypeStruct((tokens, width), BF16),
        in_specs=[VMEM, VMEM],
        out_specs=VMEM,
        scratch_shapes=[
            pltpu.VMEM((2, 3) + half, BF16),
            pltpu.VMEM((2, 2) + half, BF16),
            pltpu.VMEM((2,) + half, BF16),
            dma((2, 3)),
            dma((2, 3)),
        ],
        compiler_params=pltpu.CompilerParams(
            collective_id=1, has_side_effects=True, vmem_limit_bytes=24 * 2**20
        ),
        cost_estimate=pl.CostEstimate(flops=2**31, bytes_accessed=2**23, transcendentals=0),
        name="project",
    )(rows, weight)


def constants(groups, tokens, quota):
    slots = 2 * groups * quota
    s = np.arange(slots)
    token = np.arange(tokens)
    block = np.arange(groups)
    upto = (token[:, None] <= token[None, :]).astype(np.float32)
    lower = (block[None, :] < block[:, None]).astype(np.float32)
    col = (s[:, None] // (2 * quota) == block[None, :]).astype(np.float32)
    lane = np.arange(LANES)[None, :]
    r, half = (s % quota)[:, None], (s // quota % 2)[:, None]
    masks = []
    for p in range(2):
        masks.append(CSIZE * (lane == r) + 1.0 * (lane == quota + r) - 10000.0 * ((lane == 2 * quota) & (half != p)))
    col_mask = np.stack(masks).astype(np.float32)
    row_mask = np.ascontiguousarray(col_mask.transpose(0, 2, 1))
    as16 = lambda x: jnp.asarray(x, BF16)
    return as16(upto), as16(lower), as16(col), as16(col.T), jnp.asarray(col_mask), jnp.asarray(row_mask)


def layer(picks, location, labels, sends, groups, per_device, listed):
    planes = groups // PLANE
    full = planes // 2 - 2
    tokens = per_device * CSIZE
    quota = sends[0].shape[1] // 2
    slots = 2 * groups * quota
    dma = pltpu.SemaphoreType.DMA

    def scratch(*shape):
        return pltpu.VMEM(shape, BF16)

    widths = [heads * HD for heads in GROUPS]
    landings = [scratch(*x.shape) for x in sends]
    backs = [(groups, 2 * quota, w // 2) for w in widths]
    rings = []
    for w in widths:
        shard, block = (per_device, CSIZE, 2 * w), (CSIZE, 2 * w)
        rings += [scratch(*shard), scratch(groups, *block)]
        rings += [scratch(*shard)] * (2 * full)
        rings += [scratch(2, PLANE + PLANE // 2, *block)] * 2
        rings += [scratch(2, PLANE // 2, *block), scratch(planes * (PLANE - 1), *block)]
        rings += [dma((2, full, SUBS)), dma((2, full, SUBS)), dma((2, 3)), dma((2, 3)), dma, dma]
    return pl.pallas_call(
        functools.partial(layer_kernel, planes, listed),
        out_shape=tuple(jax.ShapeDtypeStruct(b, BF16) for b in backs),
        in_specs=[SMEM, SMEM] + [VMEM] * 10,
        out_specs=(VMEM, VMEM),
        scratch_shapes=landings
        + [
            pltpu.VMEM((PLANE, planes) + labels.shape, labels.dtype),
            pltpu.VMEM((groups, tokens), labels.dtype),
            scratch(2, slots, tokens),
            scratch(2, tokens, slots),
            scratch(per_device, CSIZE, sum(widths)),
        ]
        + [scratch(*b) for b in backs]
        + [scratch(tokens, w) for w in widths]
        + [dma((5,)), dma((5,)), dma((planes,)), dma((planes,)), dma((PLANE,)), dma((PLANE,))]
        + rings,
        compiler_params=pltpu.CompilerParams(
            collective_id=0, has_side_effects=True, vmem_limit_bytes=56 * 2**20
        ),
        cost_estimate=pl.CostEstimate(flops=2**32, bytes_accessed=2**27, transcendentals=0),
        name="layer",
    )(picks, location, labels, *sends, *constants(groups, tokens, quota))


def onehot(index, count):
    return (jnp.arange(count, dtype=jnp.int32)[:, None] == index[None, :]).astype(BF16)


def shards(query, key, value, labels, partners, out_weight):
    groups = lax.axis_size("clu")
    device = lax.axis_index("clu")
    tokens, features = query.shape
    per_device = tokens // CSIZE
    listed = partners.shape[1]
    quota = (3 * tokens + 2 * groups - 1) // (2 * groups)
    slots = groups * quota
    planes = groups // PLANE
    z, i = device // PLANE, device % PLANE

    wanted = partners.reshape(groups, per_device * listed)
    half = planes // 2
    ahead = jnp.array([0] * planes + [2, 1, -2, -1], jnp.int32)
    distance = jnp.array(list(range(planes)) + [half, half - 1, half, half + 1], jnp.int32)
    there = (z + ahead) % planes
    wanting = there[:, None] * PLANE + (i + jnp.arange(PLANE)) % PLANE
    lists = jnp.take(wanted, wanting, axis=0)
    source = ((there - distance) % planes * PLANE + i)[:, None, None]
    picks = jnp.sum(jnp.where(lists // per_device == source, lists - source * per_device, 0), axis=2)
    my_list = lax.dynamic_slice_in_dim(wanted, device, 1, 0)[0]
    from_group = my_list // per_device
    location = (z - from_group // PLANE) % planes * PLANE + from_group % PLANE

    owner = labels // per_device
    before = jnp.arange(tokens)[None, :] < jnp.arange(tokens)[:, None]
    rank = jnp.sum((owner[:, None] == owner[None, :]) & before, axis=1, dtype=jnp.int32)
    slot = owner * (2 * quota) + rank
    packer = onehot(jnp.concatenate([slot, slot + quota]), 2 * slots)
    cut = GROUPS[0] * HD

    def pack(upper, lower):
        rows = jnp.concatenate([upper, lower], axis=0)
        return exact(packer, rows).astype(BF16).reshape(groups, 2 * quota, rows.shape[1])

    sends = (
        pack(key[:, :cut], value[:, :cut]),
        pack(key[:, cut:], value[:, cut:]),
        pack(query[:, : features // 2], query[:, features // 2 :]),
    )
    returned = layer(
        picks.reshape(-1).astype(jnp.int32),
        location.astype(jnp.int32),
        labels.reshape(1, tokens),
        sends,
        groups,
        per_device,
        listed,
    )
    landed = jnp.concatenate([part.reshape(2 * slots, part.shape[2]) for part in returned], axis=1)
    token_rows = exact(packer.T, landed).astype(BF16)
    lower_cut = cut // 2
    token_rows = jnp.concatenate(
        [
            token_rows[:tokens, :lower_cut],
            token_rows[tokens:, :lower_cut],
            token_rows[:tokens, lower_cut:],
            token_rows[tokens:, lower_cut:],
        ],
        axis=1,
    )
    weight = lax.all_gather(out_weight, "clu", axis=1, tiled=True)
    return project(token_rows, weight, weight.shape[1] // lax.axis_size("head"))


def solution(mesh):
    return jax.shard_map(
        shards,
        mesh=mesh,
        in_specs=(
            P("clu", "head"),
            P("clu", "head"),
            P("clu", "head"),
            P("clu"),
            P(),
            P("head", "clu"),
        ),
        out_specs=P("clu", "head"),
        check_vma=False,
    )
```

```python
import functools
import math

import jax
import jax.numpy as jnp
import numpy as np
from jax import lax
from jax.experimental import pallas as pl
from jax.experimental.pallas import tpu as pltpu
from jax.sharding import PartitionSpec as P

HD = 128
CSIZE = 16
PLANE = 8
SUBS = 4
GROUPS = (4, 2)
LANES = 128
MESH = pl.DeviceIdType.MESH
F32 = jnp.float32
BF16 = jnp.bfloat16
VMEM = pl.BlockSpec(memory_space=pltpu.VMEM)
SMEM = pl.BlockSpec(memory_space=pltpu.SMEM)


def drain(ref, count, sem):
    some = ref.at[pl.ds(0, count)]
    pltpu.make_async_copy(some, some, sem).wait()


def exact(a, b):
    return jnp.dot(a, b, preferred_element_type=F32)


class Ring:
    def __init__(self, planes, z, i, pick, kv, out, ups, downs, packs, near, far, stage, sems):
        self.planes, self.half, self.full = planes, planes // 2, planes // 2 - 2
        self.z, self.i = z, i
        self.above = lax.rem(z + 1, planes)
        self.below = lax.rem(z + planes - 1, planes)
        self.pick, self.kv, self.out = pick, kv, out
        self.ups, self.downs = (kv,) + ups, (kv,) + downs
        self.packs, self.near, self.far, self.stage = packs, near, far, stage
        self.ring_send, self.ring_recv, self.pack_send, self.pack_recv, self.side_send, self.side_recv = sems
        self.step = kv.shape[0] // SUBS
        self.part = PLANE // 2

    def send_on(self, src, dst, send, recv, up):
        return pltpu.make_async_remote_copy(
            src_ref=src,
            dst_ref=dst,
            send_sem=send,
            recv_sem=recv,
            device_id={"z": self.above if up else self.below},
            device_id_type=MESH,
        )

    def hop(self, d, s, up):
        held = self.ups if up else self.downs
        rows = pl.ds(s * self.step, self.step)
        n = 0 if up else 1
        return self.send_on(
            held[d - 1].at[rows], held[d].at[rows], self.ring_send.at[n, d - 1, s], self.ring_recv.at[n, d - 1, s], up
        )

    def pack(self, at, up):
        n = 0 if up else 1
        rows = pl.ds(0, self.part) if at == 0 else pl.ds(self.part, PLANE)
        return self.send_on(
            self.packs.at[n, rows], self.near.at[n, rows], self.pack_send.at[n, at], self.pack_recv.at[n, at], up
        )

    def pack_on(self, up):
        n = 0 if up else 1
        return self.send_on(
            self.near.at[n, pl.ds(0, self.part)], self.far.at[n], self.pack_send.at[n, 2], self.pack_recv.at[n, 2], up
        )

    def side(self, k, j, src):
        return pltpu.make_async_remote_copy(
            src_ref=src,
            dst_ref=self.out.at[k * PLANE + self.i],
            send_sem=self.side_send,
            recv_sem=self.side_recv,
            device_id={"plane": lax.rem(self.i + j, PLANE)},
            device_id_type=MESH,
        )

    def spread(self, k, held):
        self.out[k * PLANE + self.i] = held[self.pick[k * PLANE]]
        for j in range(1, PLANE):
            at = k * (PLANE - 1) + j - 1
            self.stage[at] = held[self.pick[k * PLANE + j]]
            self.side(k, j, self.stage.at[at]).start()

    def pass_out(self, k, j, src):
        if j == 0:
            self.out[k * PLANE + self.i] = src[...]
        else:
            self.side(k, j, src).start()

    def begin(self):
        for s in range(SUBS):
            for up in (True, False):
                self.hop(1, s, up).start()
        self.spread(0, self.kv)

    def advance(self, d):
        for s in range(SUBS):
            for up in (True, False):
                self.hop(d, s, up).wait_recv()
                if d < self.full:
                    self.hop(d + 1, s, up).start()
        if d == self.full:
            for up in (True, False):
                n = 0 if up else 1
                held = (self.ups if up else self.downs)[d]
                base = (self.planes + 2 * n) * PLANE
                for j in range(self.part):
                    self.packs[n, j] = held[self.pick[base + n * self.part + j]]
                self.pack(0, up).start()
                for j in range(PLANE):
                    self.packs[n, self.part + j] = held[self.pick[base + PLANE + j]]
                self.pack(1, up).start()
        self.spread(d, self.ups[d])
        self.spread(self.planes - d, self.downs[d])

    def last_hops(self):
        for up in (True, False):
            self.pack(0, up).wait_recv()
            self.pack_on(up).start()
        for up in (True, False):
            n = 0 if up else 1
            self.pack(1, up).wait_recv()
            for j in range(PLANE):
                self.pass_out(self.full + 1 if up else self.planes - self.full - 1, j, self.near.at[n, self.part + j])
        for up in (True, False):
            n = 0 if up else 1
            self.pack_on(up).wait_recv()
            for j in range(self.part):
                self.pass_out(self.half, n * self.part + j, self.far.at[n, j])

    def arrive(self):
        drain(self.out, self.planes * (PLANE - 1), self.side_recv)

    def finish(self):
        for up in (True, False):
            for d in range(1, self.full + 1):
                for s in range(SUBS):
                    self.hop(d, s, up).wait_send()
            self.pack(0, up).wait_send()
            self.pack(1, up).wait_send()
            self.pack_on(up).wait_send()
        drain(self.stage, self.planes * (PLANE - 1), self.side_send)


def attend(listed, first, heads, loc_ref, q_ref, kv_ref, far_ref, o_ref):
    keys = (1 + listed) * CSIZE
    width = heads * HD
    scale = 1.0 / math.sqrt(HD)
    shape = (heads, 2 * CSIZE, 2 * keys)
    row, key = lax.broadcasted_iota(jnp.int32, shape, 1), lax.broadcasted_iota(jnp.int32, shape, 2)
    own = (row >= CSIZE) == (key >= keys)

    def body(pair, carry):
        tiles = []
        for c in (2 * pair, 2 * pair + 1):
            tiles.append((kv_ref, c))
            for p in range(listed):
                tiles.append((far_ref, loc_ref[c * listed + p]))
        scores = []
        for h in range(heads):
            at = (first + h) * HD
            q = jnp.concatenate([q_ref[2 * pair + n, :, at : at + HD] for n in range(2)], axis=0)
            k = jnp.concatenate([ref[at, :, h * HD : (h + 1) * HD] for ref, at in tiles], axis=0)
            scores.append(lax.dot_general(q, k, (((1,), (1,)), ((), ())), preferred_element_type=F32))
        scores = jnp.where(own, jnp.stack(scores) * scale, -jnp.inf)
        powers = jnp.exp(scores - jnp.max(scores, axis=-1, keepdims=True))
        weights = (powers / jnp.sum(powers, axis=-1, keepdims=True)).astype(BF16)
        for h in range(heads):
            v = jnp.concatenate([ref[at, :, width + h * HD : width + (h + 1) * HD] for ref, at in tiles], axis=0)
            o_ref[pl.ds(2 * CSIZE * pair, 2 * CSIZE), h * HD : (h + 1) * HD] = exact(weights[h], v).astype(BF16)
        return carry

    lax.fori_loop(0, q_ref.shape[0] // 2, body, 0)


def layer_kernel(planes, listed, *refs):
    (pick, loc, labels_ref, slot_row, slot_col, query, key, value, *rest) = refs
    (upto, lower, col, row, col_mask, row_mask, rows_out, *rest) = rest
    (send0, send1, sendq, ret0, ret1, packc, packr, arr0, arr1, arrq, all_ref, lab, dcol, drow, q_ref, back0, back1, o0, o1, *rest) = rest
    (a2a_send, a2a_recv, tag_send, tag_recv, tag_side_send, tag_side_recv, *rest) = rest
    per_ring = len(rest) // 2
    z, i = lax.axis_index("z"), lax.axis_index("plane")
    me = z * PLANE + i
    half, full, total = planes // 2, planes // 2 - 2, planes * PLANE
    hops = [half]
    for d in range(half - 1, 0, -1):
        hops += [-d, d]

    rings = []
    for g in range(2):
        kv, out, *more = rest[g * per_ring : (g + 1) * per_ring]
        ups, downs, more = tuple(more[:full]), tuple(more[full : 2 * full]), more[2 * full :]
        rings.append(Ring(planes, z, i, pick, kv, out, ups, downs, *more[:4], more[4:]))

    def at(dz, j):
        return lax.rem(z + dz + planes, planes), lax.rem(i + j, PLANE)

    barrier = pltpu.get_barrier_semaphore()

    def greet(r, carry):
        other = lax.rem(me + r, total)
        there = {"z": other // PLANE, "plane": other % PLANE}
        pl.semaphore_signal(barrier, inc=1, device_id=there, device_id_type=MESH)
        return carry

    lax.fori_loop(1, total, greet, 0)

    def to_blocks(hots, upper, lower, block):
        for l in range(0, block.shape[2], LANES):
            part = exact(hots[0], upper(l)) + exact(hots[1], lower(l))
            block[:, :, l : l + LANES] = part.reshape(total, block.shape[1], LANES).astype(BF16)

    def columns(ref, first):
        return lambda l: ref[:, first + l : first + l + LANES]

    slots, tokens = packc.shape[1], packc.shape[2]
    cut = GROUPS[0] * HD
    quota = send0.shape[1] // 2
    for p in range(2):
        number = lax.broadcasted_iota(jnp.int32, (slots, tokens), 0).astype(F32)
        packc[p] = jnp.where(number == slot_row[...] + float(p * quota), 1.0, 0.0).astype(BF16)
    to_blocks(packc, columns(key, 0), columns(value, 0), send0)
    pl.semaphore_wait(barrier, total - 1)

    def tag(dz, source):
        return pltpu.make_async_remote_copy(
            src_ref=labels_ref,
            dst_ref=all_ref.at[i, source],
            send_sem=tag_send.at[dz % planes],
            recv_sem=tag_recv.at[source],
            device_id={"z": at(dz, 0)[0]},
            device_id_type=MESH,
        )

    def tag_side(j, source):
        return pltpu.make_async_remote_copy(
            src_ref=all_ref.at[i],
            dst_ref=all_ref.at[source],
            send_sem=tag_side_send.at[j],
            recv_sem=tag_side_recv.at[source],
            device_id={"plane": at(0, j)[1]},
            device_id_type=MESH,
        )

    def exchange(n, block, landed):
        def start(to):
            pltpu.make_async_remote_copy(
                src_ref=block.at[to[0] * PLANE + to[1]],
                dst_ref=landed.at[me],
                send_sem=a2a_send.at[n],
                recv_sem=a2a_recv.at[n],
                device_id={"z": to[0], "plane": to[1]},
                device_id_type=MESH,
            ).start()

        def far(j, carry):
            for dz in hops:
                start(at(dz, j))
            return carry

        def close(j, carry):
            start(at(0, j))
            return carry

        lax.fori_loop(0, PLANE, far, 0)
        lax.fori_loop(1, PLANE, close, 0)
        landed[me] = block[me]

    def landed_all(n, landed):
        drain(landed, total - 1, a2a_recv.at[n])

    for dz in hops:
        tag(dz, z).start()
    all_ref[i, z] = labels_ref[...]
    exchange(0, send0, arr0)
    for dz in hops:
        tag(dz, lax.rem(z - dz + planes, planes)).wait_recv()
    for j in range(1, PLANE):
        tag_side(j, i).start()
    to_blocks(packc, columns(key, cut), columns(value, cut), send1)
    exchange(1, send1, arr1)
    to_blocks(packc, columns(query, 0), columns(query, query.shape[1] // 2), sendq)
    exchange(2, sendq, arrq)
    for p in range(2):
        number = lax.broadcasted_iota(jnp.int32, (tokens, slots), 1).astype(F32)
        packr[p] = jnp.where(number == slot_col[...] + float(p * quota), 1.0, 0.0).astype(BF16)
    for j in range(1, PLANE):
        tag_side(j, lax.rem(i - j + PLANE, PLANE)).wait_recv()

    for zz in range(planes):
        for ii in range(PLANE):
            lab[zz * PLANE + ii : zz * PLANE + ii + 1, :] = all_ref[ii, zz]
    per_device = q_ref.shape[0]
    local = lab[...] - me * per_device
    mine = jnp.logical_and(local >= 0, local < per_device)
    order = exact(jnp.where(mine, 1.0, 0.0).astype(BF16), upto[...])
    named = jnp.where(mine, (local + 1).astype(F32), 0.0)
    lane = lax.broadcasted_iota(jnp.int32, (total, LANES), 1)
    lanef = lane.astype(F32)
    tags, marks = [], []
    for r in range(quota):
        one = jnp.sum(jnp.where(order == r + 1.0, named, 0.0), axis=1, keepdims=True)
        one = jnp.where(one > 0.0, one - 1.0, -100.0)
        tags.append(one)
        marks.append(jnp.where(lanef == one, 1.0, 0.0))
    earlier = exact(lower[...], sum(marks).astype(BF16))
    table = jnp.where(lane == 2 * quota, 1.0, 0.0)
    for r in range(quota):
        place = jnp.sum(marks[r] * earlier, axis=1, keepdims=True)
        table = jnp.where(lane == r, tags[r], jnp.where(lane == quota + r, place, table))
        earlier = earlier + marks[r]
    wide = exact(col[...], table.astype(BF16))
    tall = exact(table.T.astype(BF16), row[...])
    for p in range(2):
        to = jnp.sum(wide * col_mask[p], axis=1, keepdims=True)
        rows = lax.broadcasted_iota(jnp.int32, (slots, tokens), 1).astype(F32)
        dcol[p] = jnp.where(rows == to, 1.0, 0.0).astype(BF16)
        to = jnp.sum(tall * row_mask[p], axis=0, keepdims=True)
        rows = lax.broadcasted_iota(jnp.int32, (tokens, slots), 0).astype(F32)
        drow[p] = jnp.where(rows == to, 1.0, 0.0).astype(BF16)

    def from_blocks(hots, landed, store):
        width = landed.shape[2]
        for l in range(0, width, LANES):
            block = landed[:, :, l : l + LANES].astype(F32).reshape(slots, LANES).astype(BF16)
            for p in range(2):
                store(p * width + l, exact(hots[p], block).astype(BF16))

    def unpack(landed, target):
        def store(at, part):
            target[:, :, at : at + LANES] = part.reshape(per_device, CSIZE, LANES)

        from_blocks(drow, landed, store)

    def give_back(n, attended, back, ret):
        to_blocks(dcol, columns(attended, 0), columns(attended, back.shape[2]), back)
        exchange(n, back, ret)

    def receive_back(n, ret, first):
        def store(at, part):
            rows_out[:, first + at : first + at + LANES] = part

        landed_all(n, ret)
        from_blocks(packr, ret, store)

    first, second = rings
    landed_all(0, arr0)
    unpack(arr0, first.kv)
    first.begin()
    for d in range(1, full + 1):
        first.advance(d)
    landed_all(1, arr1)
    unpack(arr1, second.kv)
    second.begin()
    first.last_hops()
    landed_all(2, arrq)
    unpack(arrq, q_ref)
    second.advance(1)
    first.arrive()
    attend(listed, 0, GROUPS[0], loc, q_ref, first.kv, first.out, o0)
    second.advance(2)
    give_back(3, o0, back0, ret0)
    for d in range(3, full + 1):
        second.advance(d)
    second.last_hops()
    receive_back(3, ret0, 0)
    second.arrive()
    attend(listed, GROUPS[0], GROUPS[1], loc, q_ref, second.kv, second.out, o1)
    give_back(4, o1, back1, ret1)

    for dz in hops:
        tag(dz, z).wait_send()
    for j in range(1, PLANE):
        tag_side(j, i).wait_send()
    first.finish()
    second.finish()
    for n, block in enumerate((send0, send1, sendq, back0, back1)):
        drain(block, total - 1, a2a_send.at[n])
    receive_back(4, ret1, cut)


def project_kernel(planes, rows_ref, weight_ref, order_ref, out_ref, held, sent, came, near, load, send, recv):
    n = lax.axis_size("head")
    x = lax.axis_index("head")
    left, right, opposite = lax.rem(x + n - 1, n), lax.rem(x + 1, n), lax.rem(x + 2, n)
    width = out_ref.shape[1]
    part = width // 2
    piece = width // PLANE
    owners = (opposite, right, left, x)
    for at, to in enumerate(owners):
        for p in range(PLANE):
            source = pl.multiple_of(p * (n * piece) + to * piece, piece)
            pltpu.make_async_copy(
                weight_ref.at[pl.ds(source, piece)], held.at[at, pl.ds(p * piece, piece)], load.at[at]
            ).start()

    barrier = pltpu.get_barrier_semaphore()
    for other in (left, right):
        pl.semaphore_signal(barrier, inc=1, device_id={"head": other}, device_id_type=MESH)

    def block(at, half):
        return lax.dot_general(
            rows_ref[...],
            held[at, half * part : (half + 1) * part],
            (((1,), (1,)), ((), ())),
            preferred_element_type=F32,
        )

    def ready(at):
        pltpu.make_async_copy(held.at[at], held.at[at], load.at[at]).wait()

    def copy(way, piece, src, dst):
        return pltpu.make_async_remote_copy(
            src_ref=src,
            dst_ref=dst,
            send_sem=send.at[way, piece],
            recv_sem=recv.at[way, piece],
            device_id={"head": right if way == 0 else left},
            device_id_type=MESH,
        )

    copies = []
    for w in range(2):
        copies.append([copy(w, 0, sent.at[w, 0], near.at[w])])
        copies[w] += [copy(w, p, sent.at[w, p], came.at[w, p - 1]) for p in (1, 2)]
    ready(0)
    for w in range(2):
        sent[w, 0] = block(0, w).astype(BF16)
    pl.semaphore_wait(barrier, 2)
    for w in range(2):
        copies[w][0].start()
    for w in range(2):
        ready(1 + w)
        sent[w, 1] = block(1 + w, 1 - w).astype(BF16)
        copies[w][1].start()
    summed = [block(1 + w, w) for w in range(2)]
    for w in range(2):
        copies[w][0].wait_recv()
        sent[w, 2] = (summed[w].astype(BF16).astype(F32) + near[w].astype(F32)).astype(BF16)
        copies[w][2].start()
    ready(3)
    own = [block(3, h).astype(BF16).astype(F32) for h in range(2)]
    for w in range(2):
        copies[w][1].wait_recv()
    for w in range(2):
        copies[w][2].wait_recv()
    result = jnp.zeros(out_ref.shape, F32)
    for h in range(2):
        total = own[h]
        for w in range(2):
            total = total + came[w, 1 if h == w else 0].astype(F32)
        result = result + exact(total.astype(BF16), order_ref[h * part : (h + 1) * part])
    out_ref[...] = result.astype(BF16)
    for w in range(2):
        for p in range(3):
            copies[w][p].wait_send()


def project(rows, weight, planes):
    tokens, features = rows.shape
    heads = lax.axis_size("head")
    width = weight.shape[0] // heads
    half = (tokens, width // 2)
    each = width // PLANE // (planes // heads)
    order = np.zeros((width, width), np.float32)
    for p in range(PLANE):
        for zz in range(planes // heads):
            for c in range(each):
                order[(p * (planes // heads) + zz) * each + c, (zz * PLANE + p) * each + c] = 1.0
    dma = pltpu.SemaphoreType.DMA
    return pl.pallas_call(
        functools.partial(project_kernel, planes),
        out_shape=jax.ShapeDtypeStruct((tokens, width), BF16),
        in_specs=[VMEM, pl.BlockSpec(memory_space=pl.ANY), VMEM],
        out_specs=VMEM,
        scratch_shapes=[
            pltpu.VMEM((heads, width, features), BF16),
            pltpu.VMEM((2, 3) + half, BF16),
            pltpu.VMEM((2, 2) + half, BF16),
            pltpu.VMEM((2,) + half, BF16),
            dma((heads,)),
            dma((2, 3)),
            dma((2, 3)),
        ],
        compiler_params=pltpu.CompilerParams(
            collective_id=1, has_side_effects=True, vmem_limit_bytes=60 * 2**20
        ),
        cost_estimate=pl.CostEstimate(flops=2**31, bytes_accessed=2**23, transcendentals=0),
        name="project",
    )(rows, weight, jnp.asarray(order, BF16))


def constants(groups, tokens, quota):
    slots = 2 * groups * quota
    s = np.arange(slots)
    token = np.arange(tokens)
    block = np.arange(groups)
    upto = (token[:, None] <= token[None, :]).astype(np.float32)
    lower = (block[None, :] < block[:, None]).astype(np.float32)
    col = (s[:, None] // (2 * quota) == block[None, :]).astype(np.float32)
    lane = np.arange(LANES)[None, :]
    r, half = (s % quota)[:, None], (s // quota % 2)[:, None]
    masks = []
    for p in range(2):
        masks.append(CSIZE * (lane == r) + 1.0 * (lane == quota + r) - 10000.0 * ((lane == 2 * quota) & (half != p)))
    col_mask = np.stack(masks).astype(np.float32)
    row_mask = np.ascontiguousarray(col_mask.transpose(0, 2, 1))
    as16 = lambda x: jnp.asarray(x, BF16)
    return as16(upto), as16(lower), as16(col), as16(col.T), jnp.asarray(col_mask), jnp.asarray(row_mask)


def layer(picks, location, labels, slot, query, key, value, groups, quota, listed):
    planes = groups // PLANE
    full = planes // 2 - 2
    tokens, features = query.shape
    per_device = tokens // CSIZE
    slots = 2 * groups * quota
    dma = pltpu.SemaphoreType.DMA

    def scratch(*shape):
        return pltpu.VMEM(shape, BF16)

    widths = [heads * HD for heads in GROUPS]
    sends = [scratch(groups, 2 * quota, w) for w in widths + [features // 2]]
    backs = [(groups, 2 * quota, w // 2) for w in widths]
    hots = [scratch(2, slots, tokens), scratch(2, tokens, slots)]
    rings = []
    for w in widths:
        shard, block = (per_device, CSIZE, 2 * w), (CSIZE, 2 * w)
        rings += [scratch(*shard), scratch(groups, *block)]
        rings += [scratch(*shard)] * (2 * full)
        rings += [scratch(2, PLANE + PLANE // 2, *block)] * 2
        rings += [scratch(2, PLANE // 2, *block), scratch(planes * (PLANE - 1), *block)]
        rings += [dma((2, full, SUBS)), dma((2, full, SUBS)), dma((2, 3)), dma((2, 3)), dma, dma]
    return pl.pallas_call(
        functools.partial(layer_kernel, planes, listed),
        out_shape=jax.ShapeDtypeStruct((tokens, features), BF16),
        in_specs=[SMEM, SMEM] + [VMEM] * 12,
        out_specs=VMEM,
        scratch_shapes=sends
        + [scratch(*b) for b in backs]
        + hots
        + sends
        + [
            pltpu.VMEM((PLANE, planes, 1, tokens), labels.dtype),
            pltpu.VMEM((groups, tokens), labels.dtype),
            *hots,
            scratch(per_device, CSIZE, sum(widths)),
        ]
        + [scratch(*b) for b in backs]
        + [scratch(tokens, w) for w in widths]
        + [dma((5,)), dma((5,)), dma((planes,)), dma((planes,)), dma((PLANE,)), dma((PLANE,))]
        + rings,
        compiler_params=pltpu.CompilerParams(
            collective_id=0, has_side_effects=True, vmem_limit_bytes=56 * 2**20
        ),
        cost_estimate=pl.CostEstimate(flops=2**32, bytes_accessed=2**27, transcendentals=0),
        name="layer",
    )(
        picks,
        location,
        labels.reshape(1, tokens),
        slot.reshape(1, tokens).astype(F32),
        slot.reshape(tokens, 1).astype(F32),
        query,
        key,
        value,
        *constants(groups, tokens, quota),
    )


def shards(query, key, value, labels, partners, out_weight):
    planes = lax.axis_size("z")
    groups = planes * PLANE
    z, i = lax.axis_index("z"), lax.axis_index("plane")
    device = z * PLANE + i
    tokens, features = query.shape
    per_device = tokens // CSIZE
    listed = partners.shape[1]
    quota = (3 * tokens + 2 * groups - 1) // (2 * groups)

    wanted = partners.reshape(groups, per_device * listed)
    half = planes // 2
    ahead = jnp.array([0] * planes + [2, 1, -2, -1], jnp.int32)
    distance = jnp.array(list(range(planes)) + [half, half - 1, half, half + 1], jnp.int32)
    there = (z + ahead) % planes
    wanting = there[:, None] * PLANE + (i + jnp.arange(PLANE)) % PLANE
    lists = jnp.take(wanted, wanting, axis=0)
    source = ((there - distance) % planes * PLANE + i)[:, None, None]
    picks = jnp.sum(jnp.where(lists // per_device == source, lists - source * per_device, 0), axis=2)
    my_list = lax.dynamic_slice_in_dim(wanted, device, 1, 0)[0]
    from_group = my_list // per_device
    location = (z - from_group // PLANE) % planes * PLANE + from_group % PLANE

    owner = labels // per_device
    before = jnp.arange(tokens)[None, :] < jnp.arange(tokens)[:, None]
    rank = jnp.sum((owner[:, None] == owner[None, :]) & before, axis=1, dtype=jnp.int32)
    slot = owner * (2 * quota) + rank
    token_rows = layer(
        picks.reshape(-1).astype(jnp.int32),
        location.astype(jnp.int32),
        labels,
        slot,
        query,
        key,
        value,
        groups,
        quota,
        listed,
    )
    weight = lax.all_gather(out_weight.T, "z", axis=0, tiled=True)
    weight = lax.all_gather(weight, "plane", axis=0, tiled=True)
    return project(token_rows, weight, planes)


def solution(mesh):
    heads = mesh.shape["head"]
    mesh = jax.sharding.Mesh(mesh.devices.reshape(-1, PLANE, heads), ("z", "plane", "head"))
    clu = ("z", "plane")
    return jax.shard_map(
        shards,
        mesh=mesh,
        in_specs=(
            P(clu, "head"),
            P(clu, "head"),
            P(clu, "head"),
            P(clu),
            P(),
            P("head", clu),
        ),
        out_specs=P(clu, "head"),
        check_vma=False,
    )
```

```python
import functools
import math

import jax
import jax.numpy as jnp
import numpy as np
from jax import lax
from jax.experimental import pallas as pl
from jax.experimental.pallas import tpu as pltpu
from jax.sharding import PartitionSpec as P

HD = 128
CSIZE = 16
PLANE = 8
SUBS = 4
GROUPS = (4, 2)
LANES = 128
MESH = pl.DeviceIdType.MESH
F32 = jnp.float32
BF16 = jnp.bfloat16
VMEM = pl.BlockSpec(memory_space=pltpu.VMEM)
SMEM = pl.BlockSpec(memory_space=pltpu.SMEM)


def drain(ref, count, sem):
    some = ref.at[pl.ds(0, count)]
    pltpu.make_async_copy(some, some, sem).wait()


def exact(a, b):
    return jnp.dot(a, b, preferred_element_type=F32)


class Ring:
    def __init__(self, planes, z, i, pick, kv, out, ups, downs, packs, near, far, stage, sems):
        self.planes, self.half, self.full = planes, planes // 2, planes // 2 - 2
        self.z, self.i = z, i
        self.above = lax.rem(z + 1, planes)
        self.below = lax.rem(z + planes - 1, planes)
        self.pick, self.kv, self.out = pick, kv, out
        self.ups, self.downs = (kv,) + ups, (kv,) + downs
        self.packs, self.near, self.far, self.stage = packs, near, far, stage
        self.ring_send, self.ring_recv, self.pack_send, self.pack_recv, self.side_send, self.side_recv = sems
        self.step = kv.shape[0] // SUBS
        self.part = PLANE // 2

    def send_on(self, src, dst, send, recv, up):
        return pltpu.make_async_remote_copy(
            src_ref=src,
            dst_ref=dst,
            send_sem=send,
            recv_sem=recv,
            device_id={"z": self.above if up else self.below},
            device_id_type=MESH,
        )

    def hop(self, d, s, up):
        held = self.ups if up else self.downs
        rows = pl.ds(s * self.step, self.step)
        n = 0 if up else 1
        return self.send_on(
            held[d - 1].at[rows], held[d].at[rows], self.ring_send.at[n, d - 1, s], self.ring_recv.at[n, d - 1, s], up
        )

    def pack(self, at, up):
        n = 0 if up else 1
        rows = pl.ds(0, self.part) if at == 0 else pl.ds(self.part, PLANE)
        return self.send_on(
            self.packs.at[n, rows], self.near.at[n, rows], self.pack_send.at[n, at], self.pack_recv.at[n, at], up
        )

    def pack_on(self, up):
        n = 0 if up else 1
        return self.send_on(
            self.near.at[n, pl.ds(0, self.part)], self.far.at[n], self.pack_send.at[n, 2], self.pack_recv.at[n, 2], up
        )

    def side(self, k, j, src):
        return pltpu.make_async_remote_copy(
            src_ref=src,
            dst_ref=self.out.at[k * PLANE + self.i],
            send_sem=self.side_send,
            recv_sem=self.side_recv,
            device_id={"plane": lax.rem(self.i + j, PLANE)},
            device_id_type=MESH,
        )

    def spread(self, k, held):
        self.out[k * PLANE + self.i] = held[self.pick[k * PLANE]]
        for j in range(1, PLANE):
            at = k * (PLANE - 1) + j - 1
            self.stage[at] = held[self.pick[k * PLANE + j]]
            self.side(k, j, self.stage.at[at]).start()

    def pass_out(self, k, j, src):
        if j == 0:
            self.out[k * PLANE + self.i] = src[...]
        else:
            self.side(k, j, src).start()

    def begin(self):
        for s in range(SUBS):
            for up in (True, False):
                self.hop(1, s, up).start()
        self.spread(0, self.kv)

    def advance(self, d):
        for s in range(SUBS):
            for up in (True, False):
                self.hop(d, s, up).wait_recv()
                if d < self.full:
                    self.hop(d + 1, s, up).start()
        if d == self.full:
            for up in (True, False):
                n = 0 if up else 1
                held = (self.ups if up else self.downs)[d]
                base = (self.planes + 2 * n) * PLANE
                for j in range(self.part):
                    self.packs[n, j] = held[self.pick[base + n * self.part + j]]
                self.pack(0, up).start()
                for j in range(PLANE):
                    self.packs[n, self.part + j] = held[self.pick[base + PLANE + j]]
                self.pack(1, up).start()
        self.spread(d, self.ups[d])
        self.spread(self.planes - d, self.downs[d])

    def last_hops(self):
        for up in (True, False):
            self.pack(0, up).wait_recv()
            self.pack_on(up).start()
        for up in (True, False):
            n = 0 if up else 1
            self.pack(1, up).wait_recv()
            for j in range(PLANE):
                self.pass_out(self.full + 1 if up else self.planes - self.full - 1, j, self.near.at[n, self.part + j])
        for up in (True, False):
            n = 0 if up else 1
            self.pack_on(up).wait_recv()
            for j in range(self.part):
                self.pass_out(self.half, n * self.part + j, self.far.at[n, j])

    def arrive(self):
        drain(self.out, self.planes * (PLANE - 1), self.side_recv)

    def finish(self):
        for up in (True, False):
            for d in range(1, self.full + 1):
                for s in range(SUBS):
                    self.hop(d, s, up).wait_send()
            self.pack(0, up).wait_send()
            self.pack(1, up).wait_send()
            self.pack_on(up).wait_send()
        drain(self.stage, self.planes * (PLANE - 1), self.side_send)


def attend(listed, first, heads, loc_ref, q_ref, kv_ref, far_ref, o_ref):
    keys = (1 + listed) * CSIZE
    width = heads * HD
    scale = 1.0 / math.sqrt(HD)
    shape = (heads, 2 * CSIZE, 2 * keys)
    row, key = lax.broadcasted_iota(jnp.int32, shape, 1), lax.broadcasted_iota(jnp.int32, shape, 2)
    own = (row >= CSIZE) == (key >= keys)

    def body(pair, carry):
        tiles = []
        for c in (2 * pair, 2 * pair + 1):
            tiles.append((kv_ref, c))
            for p in range(listed):
                tiles.append((far_ref, loc_ref[c * listed + p]))
        scores = []
        for h in range(heads):
            at = (first + h) * HD
            q = jnp.concatenate([q_ref[2 * pair + n, :, at : at + HD] for n in range(2)], axis=0)
            k = jnp.concatenate([ref[at, :, h * HD : (h + 1) * HD] for ref, at in tiles], axis=0)
            scores.append(lax.dot_general(q, k, (((1,), (1,)), ((), ())), preferred_element_type=F32))
        scores = jnp.where(own, jnp.stack(scores) * scale, -jnp.inf)
        powers = jnp.exp(scores - jnp.max(scores, axis=-1, keepdims=True))
        weights = (powers / jnp.sum(powers, axis=-1, keepdims=True)).astype(BF16)
        for h in range(heads):
            v = jnp.concatenate([ref[at, :, width + h * HD : width + (h + 1) * HD] for ref, at in tiles], axis=0)
            o_ref[pl.ds(2 * CSIZE * pair, 2 * CSIZE), h * HD : (h + 1) * HD] = exact(weights[h], v).astype(BF16)
        return carry

    lax.fori_loop(0, q_ref.shape[0] // 2, body, 0)


def layer_kernel(planes, heads, listed, *refs):
    (pick, loc, labels_ref, slot_row, slot_col, query, key, value, weight, *rest) = refs
    (upto, lower, col, row, col_mask, row_mask, ordered, out_ref, *rest) = rest
    (send0, send1, sendq, ret0, ret1, packc, packr, arr0, arr1, arrq, all_ref, lab, dcol, drow, q_ref, back0, back1, o0, o1, *rest) = rest
    (w_ring, w_all, rows0, rows1, total0, w_send, w_recv, w_head, w_side, t_send, t_recv, *rest) = rest
    (a2a_send, a2a_recv, tag_send, tag_recv, tag_side_send, tag_side_recv, *rest) = rest
    per_ring = len(rest) // 2
    z, i = lax.axis_index("z"), lax.axis_index("plane")
    x = lax.axis_index("head")
    me = z * PLANE + i
    half, full, total = planes // 2, planes // 2 - 2, planes * PLANE
    hops = [half]
    for d in range(half - 1, 0, -1):
        hops += [-d, d]

    rings = []
    for g in range(2):
        kv, out, *more = rest[g * per_ring : (g + 1) * per_ring]
        ups, downs, more = tuple(more[:full]), tuple(more[full : 2 * full]), more[2 * full :]
        rings.append(Ring(planes, z, i, pick, kv, out, ups, downs, *more[:4], more[4:]))

    def at(dz, j):
        return lax.rem(z + dz + planes, planes), lax.rem(i + j, PLANE)

    barrier = pltpu.get_barrier_semaphore()

    def greet(r, carry):
        other = lax.rem(me + r, total)
        there = {"z": other // PLANE, "plane": other % PLANE}
        pl.semaphore_signal(barrier, inc=1, device_id=there, device_id_type=MESH)
        return carry

    lax.fori_loop(1, total, greet, 0)
    for dx in range(1, heads):
        pl.semaphore_signal(barrier, inc=1, device_id={"head": lax.rem(x + dx, heads)}, device_id_type=MESH)
    meetings = total + heads - 2

    def to_blocks(hots, upper, lower, block):
        for l in range(0, block.shape[2], LANES):
            part = exact(hots[0], upper(l)) + exact(hots[1], lower(l))
            block[:, :, l : l + LANES] = part.reshape(total, block.shape[1], LANES).astype(BF16)

    def columns(ref, first):
        return lambda l: ref[:, first + l : first + l + LANES]

    slots, tokens = packc.shape[1], packc.shape[2]
    cut = GROUPS[0] * HD
    quota = send0.shape[1] // 2
    for p in range(2):
        number = lax.broadcasted_iota(jnp.int32, (slots, tokens), 0).astype(F32)
        packc[p] = jnp.where(number == slot_row[...] + float(p * quota), 1.0, 0.0).astype(BF16)
    to_blocks(packc, columns(key, 0), columns(value, 0), send0)
    pl.semaphore_wait(barrier, meetings)

    def tag(dz, source):
        return pltpu.make_async_remote_copy(
            src_ref=labels_ref,
            dst_ref=all_ref.at[i, source],
            send_sem=tag_send.at[dz % planes],
            recv_sem=tag_recv.at[source],
            device_id={"z": at(dz, 0)[0]},
            device_id_type=MESH,
        )

    def tag_side(j, source):
        return pltpu.make_async_remote_copy(
            src_ref=all_ref.at[i],
            dst_ref=all_ref.at[source],
            send_sem=tag_side_send.at[j],
            recv_sem=tag_side_recv.at[source],
            device_id={"plane": at(0, j)[1]},
            device_id_type=MESH,
        )

    def exchange(n, block, landed):
        def start(to):
            pltpu.make_async_remote_copy(
                src_ref=block.at[to[0] * PLANE + to[1]],
                dst_ref=landed.at[me],
                send_sem=a2a_send.at[n],
                recv_sem=a2a_recv.at[n],
                device_id={"z": to[0], "plane": to[1]},
                device_id_type=MESH,
            ).start()

        def far(j, carry):
            for dz in hops:
                start(at(dz, j))
            return carry

        def close(j, carry):
            start(at(0, j))
            return carry

        lax.fori_loop(0, PLANE, far, 0)
        lax.fori_loop(1, PLANE, close, 0)
        landed[me] = block[me]

    def landed_all(n, landed):
        drain(landed, total - 1, a2a_recv.at[n])

    def plane_at(d, up):
        return lax.rem(z + planes - d, planes) if up else lax.rem(z + d, planes)

    def weight_hop(d, up, block):
        n = 0 if up else 1
        return pltpu.make_async_remote_copy(
            src_ref=w_ring.at[block],
            dst_ref=w_ring.at[block],
            send_sem=w_send.at[n, d - 1],
            recv_sem=w_recv.at[n, d - 1],
            device_id={"z": plane_at(1, not up)},
            device_id_type=MESH,
        )

    def weight_begins():
        w_ring[z] = weight[...]
        for up in (True, False):
            weight_hop(1, up, z).start()

    def weight_goes_on(d):
        for up in (True, False):
            if d < half or up:
                weight_hop(d, up, plane_at(d, up)).wait_recv()
                if d + 1 < half or (d + 1 == half and up):
                    weight_hop(d + 1, up, plane_at(d, up)).start()

    zs = planes // heads

    def weight_head(to, source):
        return pltpu.make_async_remote_copy(
            src_ref=w_ring.at[pl.ds(to * zs, zs)],
            dst_ref=w_all.at[i, source],
            send_sem=w_head.at[0, to],
            recv_sem=w_head.at[1, source],
            device_id={"head": to},
            device_id_type=MESH,
        )

    def weight_side(j, source):
        return pltpu.make_async_remote_copy(
            src_ref=w_all.at[i],
            dst_ref=w_all.at[source],
            send_sem=w_side.at[0, j],
            recv_sem=w_side.at[1, source],
            device_id={"plane": lax.rem(i + j, PLANE)},
            device_id_type=MESH,
        )

    def rows_head(g, dx, source):
        rows = (rows0, rows1)[g]
        return pltpu.make_async_remote_copy(
            src_ref=rows.at[x],
            dst_ref=rows.at[source],
            send_sem=t_send.at[g, dx],
            recv_sem=t_recv.at[g, source],
            device_id={"head": lax.rem(x + dx, heads)},
            device_id_type=MESH,
        )

    def products(rows, first, part):
        width = rows.shape[2]
        held = PLANE // 2
        result = 0.0
        for xx in range(heads):
            block = w_all[part * held : (part + 1) * held, xx, :, :, first : first + width].astype(F32)
            block = block.reshape(block.shape[0] * block.shape[1] * block.shape[2], width).astype(BF16)
            result = result + lax.dot_general(
                rows[xx], block, (((1,), (1,)), ((), ())), preferred_element_type=F32
            )
        return result

    for dz in hops:
        tag(dz, z).start()
    all_ref[i, z] = labels_ref[...]
    weight_begins()
    exchange(0, send0, arr0)
    for dz in hops:
        tag(dz, lax.rem(z - dz + planes, planes)).wait_recv()
    for j in range(1, PLANE):
        tag_side(j, i).start()
    to_blocks(packc, columns(key, cut), columns(value, cut), send1)
    weight_goes_on(1)
    exchange(1, send1, arr1)
    to_blocks(packc, columns(query, 0), columns(query, query.shape[1] // 2), sendq)
    weight_goes_on(2)
    exchange(2, sendq, arrq)
    for p in range(2):
        number = lax.broadcasted_iota(jnp.int32, (tokens, slots), 1).astype(F32)
        packr[p] = jnp.where(number == slot_col[...] + float(p * quota), 1.0, 0.0).astype(BF16)
    for j in range(1, PLANE):
        tag_side(j, lax.rem(i - j + PLANE, PLANE)).wait_recv()

    for zz in range(planes):
        for ii in range(PLANE):
            lab[zz * PLANE + ii : zz * PLANE + ii + 1, :] = all_ref[ii, zz]
    per_device = q_ref.shape[0]
    local = lab[...] - me * per_device
    mine = jnp.logical_and(local >= 0, local < per_device)
    order = exact(jnp.where(mine, 1.0, 0.0).astype(BF16), upto[...])
    named = jnp.where(mine, (local + 1).astype(F32), 0.0)
    lane = lax.broadcasted_iota(jnp.int32, (total, LANES), 1)
    lanef = lane.astype(F32)
    tags, marks = [], []
    for r in range(quota):
        one = jnp.sum(jnp.where(order == r + 1.0, named, 0.0), axis=1, keepdims=True)
        one = jnp.where(one > 0.0, one - 1.0, -100.0)
        tags.append(one)
        marks.append(jnp.where(lanef == one, 1.0, 0.0))
    earlier = exact(lower[...], sum(marks).astype(BF16))
    table = jnp.where(lane == 2 * quota, 1.0, 0.0)
    for r in range(quota):
        place = jnp.sum(marks[r] * earlier, axis=1, keepdims=True)
        table = jnp.where(lane == r, tags[r], jnp.where(lane == quota + r, place, table))
        earlier = earlier + marks[r]
    wide = exact(col[...], table.astype(BF16))
    tall = exact(table.T.astype(BF16), row[...])
    for p in range(2):
        to = jnp.sum(wide * col_mask[p], axis=1, keepdims=True)
        rows = lax.broadcasted_iota(jnp.int32, (slots, tokens), 1).astype(F32)
        dcol[p] = jnp.where(rows == to, 1.0, 0.0).astype(BF16)
        to = jnp.sum(tall * row_mask[p], axis=0, keepdims=True)
        rows = lax.broadcasted_iota(jnp.int32, (tokens, slots), 0).astype(F32)
        drow[p] = jnp.where(rows == to, 1.0, 0.0).astype(BF16)

    def from_blocks(hots, landed, store):
        width = landed.shape[2]
        for l in range(0, width, LANES):
            block = landed[:, :, l : l + LANES].astype(F32).reshape(slots, LANES).astype(BF16)
            for p in range(2):
                store(p * width + l, exact(hots[p], block).astype(BF16))

    def unpack(landed, target):
        def store(at, part):
            target[:, :, at : at + LANES] = part.reshape(per_device, CSIZE, LANES)

        from_blocks(drow, landed, store)

    def give_back(n, attended, back, ret):
        to_blocks(dcol, columns(attended, 0), columns(attended, back.shape[2]), back)
        exchange(n, back, ret)

    def receive_back(n, ret, g):
        rows = (rows0, rows1)[g]

        def store(at, part):
            rows[x, :, at : at + LANES] = part

        landed_all(n, ret)
        from_blocks(packr, ret, store)
        for dx in range(1, heads):
            rows_head(g, dx, x).start()

    def rows_gathered(g):
        for dx in range(1, heads):
            rows_head(g, dx, lax.rem(x + heads - dx, heads)).wait_recv()

    first, second = rings
    landed_all(0, arr0)
    unpack(arr0, first.kv)
    first.begin()
    weight_goes_on(3)
    for d in range(1, full + 1):
        first.advance(d)
        if d + 3 <= half:
            weight_goes_on(d + 3)
        if d + 3 == half:
            w_all[i, x] = w_ring[pl.ds(x * zs, zs)]
            for dx in range(1, heads):
                weight_head(lax.rem(x + dx, heads), x).start()
    for dx in range(1, heads):
        weight_head(x, lax.rem(x + dx, heads)).wait_recv()
    for j in range(1, PLANE):
        weight_side(j, i).start()
    landed_all(1, arr1)
    unpack(arr1, second.kv)
    second.begin()
    first.last_hops()
    landed_all(2, arrq)
    unpack(arrq, q_ref)
    second.advance(1)
    first.arrive()
    attend(listed, 0, GROUPS[0], loc, q_ref, first.kv, first.out, o0)
    second.advance(2)
    give_back(3, o0, back0, ret0)
    for d in range(3, full + 1):
        second.advance(d)
    second.last_hops()
    receive_back(3, ret0, 0)
    second.arrive()
    attend(listed, GROUPS[0], GROUPS[1], loc, q_ref, second.kv, second.out, o1)
    give_back(4, o1, back1, ret1)
    for j in range(1, PLANE):
        weight_side(j, lax.rem(i + PLANE - j, PLANE)).wait_recv()
    rows_gathered(0)
    part = out_ref.shape[1] // 2
    for p in range(2):
        total0[:, p * part : (p + 1) * part] = products(rows0, 0, p)

    for dz in hops:
        tag(dz, z).wait_send()
    for j in range(1, PLANE):
        tag_side(j, i).wait_send()
        weight_side(j, i).wait_send()
    for up in (True, False):
        for d in range(1, half + 1):
            if d < half or up:
                weight_hop(d, up, z).wait_send()
    for dx in range(1, heads):
        weight_head(lax.rem(x + dx, heads), x).wait_send()
        rows_head(0, dx, x).wait_send()
    first.finish()
    second.finish()
    for n, block in enumerate((send0, send1, sendq, back0)):
        drain(block, total - 1, a2a_send.at[n])
    receive_back(4, ret1, 1)
    drain(back1, total - 1, a2a_send.at[4])
    rows_gathered(1)
    result = 0.0
    for p in range(2):
        summed = (total0[:, p * part : (p + 1) * part] + products(rows1, cut, p)).astype(BF16)
        result = result + exact(summed, ordered[p * part : (p + 1) * part])
    out_ref[...] = result.astype(BF16)
    for dx in range(1, heads):
        rows_head(1, dx, x).wait_send()


def constants(groups, tokens, quota):
    slots = 2 * groups * quota
    s = np.arange(slots)
    token = np.arange(tokens)
    block = np.arange(groups)
    upto = (token[:, None] <= token[None, :]).astype(np.float32)
    lower = (block[None, :] < block[:, None]).astype(np.float32)
    col = (s[:, None] // (2 * quota) == block[None, :]).astype(np.float32)
    lane = np.arange(LANES)[None, :]
    r, half = (s % quota)[:, None], (s // quota % 2)[:, None]
    masks = []
    for p in range(2):
        masks.append(CSIZE * (lane == r) + 1.0 * (lane == quota + r) - 10000.0 * ((lane == 2 * quota) & (half != p)))
    col_mask = np.stack(masks).astype(np.float32)
    row_mask = np.ascontiguousarray(col_mask.transpose(0, 2, 1))
    as16 = lambda x: jnp.asarray(x, BF16)
    return as16(upto), as16(lower), as16(col), as16(col.T), jnp.asarray(col_mask), jnp.asarray(row_mask)


def column_order(planes, heads, width):
    zs = planes // heads
    each = width // PLANE // zs
    order = np.zeros((width, width), np.float32)
    for p in range(PLANE):
        for zz in range(zs):
            for c in range(each):
                order[(p * zs + zz) * each + c, (zz * PLANE + p) * each + c] = 1.0
    return jnp.asarray(order, BF16)


def layer(picks, location, labels, slot, query, key, value, weight, groups, heads, quota, listed):
    planes = groups // PLANE
    full = planes // 2 - 2
    tokens, features = query.shape
    per_device = tokens // CSIZE
    slots = 2 * groups * quota
    dma = pltpu.SemaphoreType.DMA

    def scratch(*shape):
        return pltpu.VMEM(shape, BF16)

    widths = [heads * HD for heads in GROUPS]
    each = weight.shape[0]
    width = each * groups // heads
    zs = planes // heads
    sends = [scratch(groups, 2 * quota, w) for w in widths + [features // 2]]
    backs = [(groups, 2 * quota, w // 2) for w in widths]
    hots = [scratch(2, slots, tokens), scratch(2, tokens, slots)]
    rings = []
    for w in widths:
        shard, block = (per_device, CSIZE, 2 * w), (CSIZE, 2 * w)
        rings += [scratch(*shard), scratch(groups, *block)]
        rings += [scratch(*shard)] * (2 * full)
        rings += [scratch(2, PLANE + PLANE // 2, *block)] * 2
        rings += [scratch(2, PLANE // 2, *block), scratch(planes * (PLANE - 1), *block)]
        rings += [dma((2, full, SUBS)), dma((2, full, SUBS)), dma((2, 3)), dma((2, 3)), dma, dma]
    return pl.pallas_call(
        functools.partial(layer_kernel, planes, heads, listed),
        out_shape=jax.ShapeDtypeStruct((tokens, width), BF16),
        in_specs=[SMEM, SMEM] + [VMEM] * 14,
        out_specs=VMEM,
        scratch_shapes=sends
        + [scratch(*b) for b in backs]
        + hots
        + sends
        + [
            pltpu.VMEM((PLANE, planes, 1, tokens), labels.dtype),
            pltpu.VMEM((groups, tokens), labels.dtype),
            *hots,
            scratch(per_device, CSIZE, sum(widths)),
        ]
        + [scratch(*b) for b in backs]
        + [scratch(tokens, w) for w in widths]
        + [
            scratch(planes, each, features),
            scratch(PLANE, heads, zs, each, features),
        ]
        + [scratch(heads, tokens, w) for w in widths]
        + [
            pltpu.VMEM((tokens, width), F32),
            dma((2, planes // 2)),
            dma((2, planes // 2)),
            dma((2, heads)),
            dma((2, PLANE)),
            dma((2, heads)),
            dma((2, heads)),
        ]
        + [dma((5,)), dma((5,)), dma((planes,)), dma((planes,)), dma((PLANE,)), dma((PLANE,))]
        + rings,
        compiler_params=pltpu.CompilerParams(
            collective_id=0, has_side_effects=True, vmem_limit_bytes=61 * 2**20
        ),
        cost_estimate=pl.CostEstimate(flops=2**32, bytes_accessed=2**27, transcendentals=0),
        name="layer",
    )(
        picks,
        location,
        labels.reshape(1, tokens),
        slot.reshape(1, tokens).astype(F32),
        slot.reshape(tokens, 1).astype(F32),
        query,
        key,
        value,
        weight,
        *constants(groups, tokens, quota),
        column_order(planes, heads, width),
    )


def shards(query, key, value, labels, partners, out_weight):
    planes = lax.axis_size("z")
    groups = planes * PLANE
    z, i = lax.axis_index("z"), lax.axis_index("plane")
    device = z * PLANE + i
    tokens, features = query.shape
    per_device = tokens // CSIZE
    listed = partners.shape[1]
    quota = (3 * tokens + 2 * groups - 1) // (2 * groups)

    wanted = partners.reshape(groups, per_device * listed)
    half = planes // 2
    ahead = jnp.array([0] * planes + [2, 1, -2, -1], jnp.int32)
    distance = jnp.array(list(range(planes)) + [half, half - 1, half, half + 1], jnp.int32)
    there = (z + ahead) % planes
    wanting = there[:, None] * PLANE + (i + jnp.arange(PLANE)) % PLANE
    lists = jnp.take(wanted, wanting, axis=0)
    source = ((there - distance) % planes * PLANE + i)[:, None, None]
    picks = jnp.sum(jnp.where(lists // per_device == source, lists - source * per_device, 0), axis=2)
    my_list = lax.dynamic_slice_in_dim(wanted, device, 1, 0)[0]
    from_group = my_list // per_device
    location = (z - from_group // PLANE) % planes * PLANE + from_group % PLANE

    owner = labels // per_device
    before = jnp.arange(tokens)[None, :] < jnp.arange(tokens)[:, None]
    rank = jnp.sum((owner[:, None] == owner[None, :]) & before, axis=1, dtype=jnp.int32)
    slot = owner * (2 * quota) + rank
    return layer(
        picks.reshape(-1).astype(jnp.int32),
        location.astype(jnp.int32),
        labels,
        slot,
        query,
        key,
        value,
        out_weight.T,
        groups,
        lax.axis_size("head"),
        quota,
        listed,
    )


def solution(mesh):
    heads = mesh.shape["head"]
    mesh = jax.sharding.Mesh(mesh.devices.reshape(-1, PLANE, heads), ("z", "plane", "head"))
    clu = ("z", "plane")
    return jax.shard_map(
        shards,
        mesh=mesh,
        in_specs=(
            P(clu, "head"),
            P(clu, "head"),
            P(clu, "head"),
            P(clu),
            P(),
            P("head", clu),
        ),
        out_specs=P(clu, "head"),
        check_vma=False,
    )
```

```python
import functools
import math

import jax
import jax.numpy as jnp
import numpy as np
from jax import lax
from jax.experimental import pallas as pl
from jax.experimental.pallas import tpu as pltpu
from jax.sharding import PartitionSpec as P

HD = 128
CSIZE = 16
PLANE = 8
SUBS = 4
GROUPS = (4, 2)
LANES = 128
MESH = pl.DeviceIdType.MESH
F32 = jnp.float32
BF16 = jnp.bfloat16
VMEM = pl.BlockSpec(memory_space=pltpu.VMEM)
SMEM = pl.BlockSpec(memory_space=pltpu.SMEM)


def drain(ref, count, sem):
    some = ref.at[pl.ds(0, count)]
    pltpu.make_async_copy(some, some, sem).wait()


def exact(a, b):
    return jnp.dot(a, b, preferred_element_type=F32)


class Ring:
    def __init__(self, planes, z, i, pick, kv, out, ups, downs, packs, near, far, stage, sems):
        self.planes, self.half, self.full = planes, planes // 2, planes // 2 - 2
        self.z, self.i = z, i
        self.above = lax.rem(z + 1, planes)
        self.below = lax.rem(z + planes - 1, planes)
        self.pick, self.kv, self.out = pick, kv, out
        self.ups, self.downs = (kv,) + ups, (kv,) + downs
        self.packs, self.near, self.far, self.stage = packs, near, far, stage
        self.ring_send, self.ring_recv, self.pack_send, self.pack_recv, self.side_send, self.side_recv = sems
        self.step = kv.shape[0] // SUBS
        self.part = PLANE // 2

    def send_on(self, src, dst, send, recv, up):
        return pltpu.make_async_remote_copy(
            src_ref=src,
            dst_ref=dst,
            send_sem=send,
            recv_sem=recv,
            device_id={"z": self.above if up else self.below},
            device_id_type=MESH,
        )

    def hop(self, d, s, up):
        held = self.ups if up else self.downs
        rows = pl.ds(s * self.step, self.step)
        n = 0 if up else 1
        return self.send_on(
            held[d - 1].at[rows], held[d].at[rows], self.ring_send.at[n, d - 1, s], self.ring_recv.at[n, d - 1, s], up
        )

    def pack(self, at, up):
        n = 0 if up else 1
        rows = pl.ds(0, self.part) if at == 0 else pl.ds(self.part, PLANE)
        return self.send_on(
            self.packs.at[n, rows], self.near.at[n, rows], self.pack_send.at[n, at], self.pack_recv.at[n, at], up
        )

    def pack_on(self, up):
        n = 0 if up else 1
        return self.send_on(
            self.near.at[n, pl.ds(0, self.part)], self.far.at[n], self.pack_send.at[n, 2], self.pack_recv.at[n, 2], up
        )

    def side(self, k, j, src):
        return pltpu.make_async_remote_copy(
            src_ref=src,
            dst_ref=self.out.at[k * PLANE + self.i],
            send_sem=self.side_send,
            recv_sem=self.side_recv,
            device_id={"plane": lax.rem(self.i + j, PLANE)},
            device_id_type=MESH,
        )

    def spread(self, k, held):
        self.out[k * PLANE + self.i] = held[self.pick[k * PLANE]]
        for j in range(1, PLANE):
            at = k * (PLANE - 1) + j - 1
            self.stage[at] = held[self.pick[k * PLANE + j]]
            self.side(k, j, self.stage.at[at]).start()

    def pass_out(self, k, j, src):
        if j == 0:
            self.out[k * PLANE + self.i] = src[...]
        else:
            self.side(k, j, src).start()

    def begin(self):
        for s in range(SUBS):
            for up in (True, False):
                self.hop(1, s, up).start()
        self.spread(0, self.kv)

    def advance(self, d):
        for s in range(SUBS):
            for up in (True, False):
                self.hop(d, s, up).wait_recv()
                if d < self.full:
                    self.hop(d + 1, s, up).start()
        if d == self.full:
            for up in (True, False):
                n = 0 if up else 1
                held = (self.ups if up else self.downs)[d]
                base = (self.planes + 2 * n) * PLANE
                for j in range(self.part):
                    self.packs[n, j] = held[self.pick[base + n * self.part + j]]
                self.pack(0, up).start()
                for j in range(PLANE):
                    self.packs[n, self.part + j] = held[self.pick[base + PLANE + j]]
                self.pack(1, up).start()
        self.spread(d, self.ups[d])
        self.spread(self.planes - d, self.downs[d])

    def last_hops(self):
        for up in (True, False):
            self.pack(0, up).wait_recv()
            self.pack_on(up).start()
        for up in (True, False):
            n = 0 if up else 1
            self.pack(1, up).wait_recv()
            for j in range(PLANE):
                self.pass_out(self.full + 1 if up else self.planes - self.full - 1, j, self.near.at[n, self.part + j])
        for up in (True, False):
            n = 0 if up else 1
            self.pack_on(up).wait_recv()
            for j in range(self.part):
                self.pass_out(self.half, n * self.part + j, self.far.at[n, j])

    def arrive(self):
        drain(self.out, self.planes * (PLANE - 1), self.side_recv)

    def finish(self):
        for up in (True, False):
            for d in range(1, self.full + 1):
                for s in range(SUBS):
                    self.hop(d, s, up).wait_send()
            self.pack(0, up).wait_send()
            self.pack(1, up).wait_send()
            self.pack_on(up).wait_send()
        drain(self.stage, self.planes * (PLANE - 1), self.side_send)


def attend(listed, first, heads, loc_ref, q_ref, kv_ref, far_ref, o_ref):
    keys = (1 + listed) * CSIZE
    width = heads * HD
    scale = 1.0 / math.sqrt(HD)
    shape = (heads, 2 * CSIZE, 2 * keys)
    row, key = lax.broadcasted_iota(jnp.int32, shape, 1), lax.broadcasted_iota(jnp.int32, shape, 2)
    own = (row >= CSIZE) == (key >= keys)

    def body(pair, carry):
        tiles = []
        for c in (2 * pair, 2 * pair + 1):
            tiles.append((kv_ref, c))
            for p in range(listed):
                tiles.append((far_ref, loc_ref[c * listed + p]))
        scores = []
        for h in range(heads):
            at = (first + h) * HD
            q = jnp.concatenate([q_ref[2 * pair + n, :, at : at + HD] for n in range(2)], axis=0)
            k = jnp.concatenate([ref[at, :, h * HD : (h + 1) * HD] for ref, at in tiles], axis=0)
            scores.append(lax.dot_general(q, k, (((1,), (1,)), ((), ())), preferred_element_type=F32))
        scores = jnp.where(own, jnp.stack(scores) * scale, -jnp.inf)
        powers = jnp.exp(scores - jnp.max(scores, axis=-1, keepdims=True))
        weights = (powers / jnp.sum(powers, axis=-1, keepdims=True)).astype(BF16)
        for h in range(heads):
            v = jnp.concatenate([ref[at, :, width + h * HD : width + (h + 1) * HD] for ref, at in tiles], axis=0)
            o_ref[pl.ds(2 * CSIZE * pair, 2 * CSIZE), h * HD : (h + 1) * HD] = exact(weights[h], v).astype(BF16)
        return carry

    lax.fori_loop(0, q_ref.shape[0] // 2, body, 0)


def layer_kernel(planes, heads, listed, *refs):
    (pick, loc, labels_ref, slot_row, slot_col, query, key, value, weight, *rest) = refs
    (upto, lower, col, row, col_mask, row_mask, ordered, out_ref, *rest) = rest
    (send0, send1, sendq, ret0, ret1, packc, packr, arr0, arr1, arrq, all_ref, lab, dcol, drow, q_ref, back0, back1, o0, o1, *rest) = rest
    (w_ring, w_all, rows0, rows1, total0, w_send, w_recv, w_head, w_chip_send, w_chip_recv, w_core_send, w_core_recv, t_send, t_recv, *rest) = rest
    (a2a_send, a2a_recv, tag_send, tag_recv, tag_side_send, tag_side_recv, *rest) = rest
    per_ring = len(rest) // 2
    z, i = lax.axis_index("z"), lax.axis_index("plane")
    x = lax.axis_index("head")
    me = z * PLANE + i
    half, full, total = planes // 2, planes // 2 - 2, planes * PLANE
    hops = [half]
    for d in range(half - 1, 0, -1):
        hops += [-d, d]

    rings = []
    for g in range(2):
        kv, out, *more = rest[g * per_ring : (g + 1) * per_ring]
        ups, downs, more = tuple(more[:full]), tuple(more[full : 2 * full]), more[2 * full :]
        rings.append(Ring(planes, z, i, pick, kv, out, ups, downs, *more[:4], more[4:]))

    def at(dz, j):
        return lax.rem(z + dz + planes, planes), lax.rem(i + j, PLANE)

    barrier = pltpu.get_barrier_semaphore()

    def greet(r, carry):
        other = lax.rem(me + r, total)
        there = {"z": other // PLANE, "plane": other % PLANE}
        pl.semaphore_signal(barrier, inc=1, device_id=there, device_id_type=MESH)
        return carry

    lax.fori_loop(1, total, greet, 0)
    for dx in range(1, heads):
        pl.semaphore_signal(barrier, inc=1, device_id={"head": lax.rem(x + dx, heads)}, device_id_type=MESH)
    meetings = total + heads - 2

    def to_blocks(hots, upper, lower, block):
        for l in range(0, block.shape[2], LANES):
            part = exact(hots[0], upper(l)) + exact(hots[1], lower(l))
            block[:, :, l : l + LANES] = part.reshape(total, block.shape[1], LANES).astype(BF16)

    def columns(ref, first):
        return lambda l: ref[:, first + l : first + l + LANES]

    slots, tokens = packc.shape[1], packc.shape[2]
    cut = GROUPS[0] * HD
    quota = send0.shape[1] // 2
    for p in range(2):
        number = lax.broadcasted_iota(jnp.int32, (slots, tokens), 0).astype(F32)
        packc[p] = jnp.where(number == slot_row[...] + float(p * quota), 1.0, 0.0).astype(BF16)
    to_blocks(packc, columns(key, 0), columns(value, 0), send0)
    pl.semaphore_wait(barrier, meetings)

    def tag(dz, source):
        return pltpu.make_async_remote_copy(
            src_ref=labels_ref,
            dst_ref=all_ref.at[i, source],
            send_sem=tag_send.at[dz % planes],
            recv_sem=tag_recv.at[source],
            device_id={"z": at(dz, 0)[0]},
            device_id_type=MESH,
        )

    def tag_side(j, source):
        return pltpu.make_async_remote_copy(
            src_ref=all_ref.at[i],
            dst_ref=all_ref.at[source],
            send_sem=tag_side_send.at[j],
            recv_sem=tag_side_recv.at[source],
            device_id={"plane": at(0, j)[1]},
            device_id_type=MESH,
        )

    def exchange(n, block, landed, between=None):
        def start(to):
            pltpu.make_async_remote_copy(
                src_ref=block.at[to[0] * PLANE + to[1]],
                dst_ref=landed.at[me],
                send_sem=a2a_send.at[n],
                recv_sem=a2a_recv.at[n],
                device_id={"z": to[0], "plane": to[1]},
                device_id_type=MESH,
            ).start()

        def far(j, carry):
            for dz in hops:
                start(at(dz, j))
            return carry

        def close(j, carry):
            start(at(0, j))
            return carry

        if between is None:
            lax.fori_loop(0, PLANE, far, 0)
        else:
            lax.fori_loop(0, PLANE // 2, far, 0)
            between()
            lax.fori_loop(PLANE // 2, PLANE, far, 0)
        lax.fori_loop(1, PLANE, close, 0)
        landed[me] = block[me]

    def landed_all(n, landed):
        drain(landed, total - 1, a2a_recv.at[n])

    def plane_at(d, up):
        return lax.rem(z + planes - d, planes) if up else lax.rem(z + d, planes)

    def weight_hop(d, up, block):
        n = 0 if up else 1
        return pltpu.make_async_remote_copy(
            src_ref=w_ring.at[block],
            dst_ref=w_ring.at[block],
            send_sem=w_send.at[n, d - 1],
            recv_sem=w_recv.at[n, d - 1],
            device_id={"z": plane_at(1, not up)},
            device_id_type=MESH,
        )

    def weight_begins():
        w_ring[z] = weight[...]
        for up in (True, False):
            weight_hop(1, up, z).start()

    def weight_goes_on(d):
        for up in (True, False):
            if d < half or up:
                weight_hop(d, up, plane_at(d, up)).wait_recv()
                if d + 1 < half or (d + 1 == half and up):
                    weight_hop(d + 1, up, plane_at(d, up)).start()

    zs = planes // heads

    def weight_head(to, source):
        return pltpu.make_async_remote_copy(
            src_ref=w_ring.at[pl.ds(to * zs, zs)],
            dst_ref=w_all.at[i, source],
            send_sem=w_head.at[0, to],
            recv_sem=w_head.at[1, source],
            device_id={"head": to},
            device_id_type=MESH,
        )

    chips = PLANE // 2
    sibling = i + 1 - 2 * (i % 2)

    def of_set(c):
        return lax.rem(x + c, heads)

    def weight_chip(c, m, source):
        return pltpu.make_async_remote_copy(
            src_ref=w_all.at[i, of_set(c)],
            dst_ref=w_all.at[source, of_set(c)],
            send_sem=w_chip_send.at[c, m],
            recv_sem=w_chip_recv.at[c, m],
            device_id={"plane": lax.rem(i + 2 * m, PLANE)},
            device_id_type=MESH,
        )

    def weight_core(c, m, first):
        at = lax.rem(first + 2 * m, PLANE)
        return pltpu.make_async_remote_copy(
            src_ref=w_all.at[at, of_set(c)],
            dst_ref=w_all.at[at, of_set(c)],
            send_sem=w_core_send.at[c, m],
            recv_sem=w_core_recv.at[c, m],
            device_id={"plane": sibling},
            device_id_type=MESH,
        )

    def weight_to_chips(c):
        for m in range(1, chips):
            weight_chip(c, m, i).start()
        weight_core(c, 0, i).start()

    def weight_to_core(c):
        for m in range(1, chips):
            weight_chip(c, m, lax.rem(i + PLANE - 2 * m, PLANE)).wait_recv()
        for m in range(1, chips):
            weight_core(c, m, i).start()

    def rows_head(g, dx, source):
        rows = (rows0, rows1)[g]
        return pltpu.make_async_remote_copy(
            src_ref=rows.at[x],
            dst_ref=rows.at[source],
            send_sem=t_send.at[g, dx],
            recv_sem=t_recv.at[g, source],
            device_id={"head": lax.rem(x + dx, heads)},
            device_id_type=MESH,
        )

    def products(rows, first, part):
        width = rows.shape[2]
        held = PLANE // 2
        result = 0.0
        for xx in range(heads):
            block = w_all[part * held : (part + 1) * held, xx, :, :, first : first + width].astype(F32)
            block = block.reshape(block.shape[0] * block.shape[1] * block.shape[2], width).astype(BF16)
            result = result + lax.dot_general(
                rows[xx], block, (((1,), (1,)), ((), ())), preferred_element_type=F32
            )
        return result

    for dz in hops:
        tag(dz, z).start()
    all_ref[i, z] = labels_ref[...]
    weight_begins()
    exchange(0, send0, arr0, lambda: weight_goes_on(1))
    for dz in hops:
        tag(dz, lax.rem(z - dz + planes, planes)).wait_recv()
    for j in range(1, PLANE):
        tag_side(j, i).start()
    to_blocks(packc, columns(key, cut), columns(value, cut), send1)
    weight_goes_on(2)
    exchange(1, send1, arr1)
    to_blocks(packc, columns(query, 0), columns(query, query.shape[1] // 2), sendq)
    weight_goes_on(3)
    exchange(2, sendq, arrq, lambda: weight_goes_on(4))
    for p in range(2):
        number = lax.broadcasted_iota(jnp.int32, (tokens, slots), 1).astype(F32)
        packr[p] = jnp.where(number == slot_col[...] + float(p * quota), 1.0, 0.0).astype(BF16)
    for j in range(1, PLANE):
        tag_side(j, lax.rem(i - j + PLANE, PLANE)).wait_recv()

    for zz in range(planes):
        for ii in range(PLANE):
            lab[zz * PLANE + ii : zz * PLANE + ii + 1, :] = all_ref[ii, zz]
    per_device = q_ref.shape[0]
    local = lab[...] - me * per_device
    mine = jnp.logical_and(local >= 0, local < per_device)
    order = exact(jnp.where(mine, 1.0, 0.0).astype(BF16), upto[...])
    named = jnp.where(mine, (local + 1).astype(F32), 0.0)
    lane = lax.broadcasted_iota(jnp.int32, (total, LANES), 1)
    lanef = lane.astype(F32)
    tags, marks = [], []
    for r in range(quota):
        one = jnp.sum(jnp.where(order == r + 1.0, named, 0.0), axis=1, keepdims=True)
        one = jnp.where(one > 0.0, one - 1.0, -100.0)
        tags.append(one)
        marks.append(jnp.where(lanef == one, 1.0, 0.0))
    earlier = exact(lower[...], sum(marks).astype(BF16))
    table = jnp.where(lane == 2 * quota, 1.0, 0.0)
    for r in range(quota):
        place = jnp.sum(marks[r] * earlier, axis=1, keepdims=True)
        table = jnp.where(lane == r, tags[r], jnp.where(lane == quota + r, place, table))
        earlier = earlier + marks[r]
    wide = exact(col[...], table.astype(BF16))
    tall = exact(table.T.astype(BF16), row[...])
    for p in range(2):
        to = jnp.sum(wide * col_mask[p], axis=1, keepdims=True)
        rows = lax.broadcasted_iota(jnp.int32, (slots, tokens), 1).astype(F32)
        dcol[p] = jnp.where(rows == to, 1.0, 0.0).astype(BF16)
        to = jnp.sum(tall * row_mask[p], axis=0, keepdims=True)
        rows = lax.broadcasted_iota(jnp.int32, (tokens, slots), 0).astype(F32)
        drow[p] = jnp.where(rows == to, 1.0, 0.0).astype(BF16)

    def from_blocks(hots, landed, store):
        width = landed.shape[2]
        for l in range(0, width, LANES):
            block = landed[:, :, l : l + LANES].astype(F32).reshape(slots, LANES).astype(BF16)
            for p in range(2):
                store(p * width + l, exact(hots[p], block).astype(BF16))

    def unpack(landed, target):
        def store(at, part):
            target[:, :, at : at + LANES] = part.reshape(per_device, CSIZE, LANES)

        from_blocks(drow, landed, store)

    def give_back(n, attended, back, ret):
        to_blocks(dcol, columns(attended, 0), columns(attended, back.shape[2]), back)
        exchange(n, back, ret)

    def receive_back(n, ret, g):
        rows = (rows0, rows1)[g]

        def store(at, part):
            rows[x, :, at : at + LANES] = part

        landed_all(n, ret)
        from_blocks(packr, ret, store)
        for dx in range(1, heads):
            rows_head(g, dx, x).start()

    def rows_gathered(g):
        for dx in range(1, heads):
            rows_head(g, dx, lax.rem(x + heads - dx, heads)).wait_recv()

    first, second = rings
    landed_all(0, arr0)
    unpack(arr0, first.kv)
    first.begin()
    weight_goes_on(5)
    for d in range(1, full + 1):
        first.advance(d)
        if d + 5 <= half:
            weight_goes_on(d + 5)
        if d + 5 == half:
            w_all[i, x] = w_ring[pl.ds(x * zs, zs)]
            for dx in range(1, heads):
                weight_head(lax.rem(x + dx, heads), x).start()
            weight_to_chips(0)
        if d + 5 > half:
            c = d + 5 - half
            weight_head(x, of_set(c)).wait_recv()
            weight_to_chips(c)
    landed_all(1, arr1)
    unpack(arr1, second.kv)
    second.begin()
    first.last_hops()
    landed_all(2, arrq)
    unpack(arrq, q_ref)
    second.advance(1)
    weight_to_core(0)
    weight_to_core(1)
    first.arrive()
    attend(listed, 0, GROUPS[0], loc, q_ref, first.kv, first.out, o0)
    second.advance(2)
    give_back(3, o0, back0, ret0)
    for d in range(3, full + 1):
        second.advance(d)
        if d - 1 < heads:
            weight_to_core(d - 1)
    second.last_hops()
    receive_back(3, ret0, 0)
    second.arrive()
    attend(listed, GROUPS[0], GROUPS[1], loc, q_ref, second.kv, second.out, o1)
    give_back(4, o1, back1, ret1)
    for c in range(heads):
        for m in range(chips):
            weight_core(c, m, sibling).wait_recv()
    rows_gathered(0)
    part = out_ref.shape[1] // 2
    for p in range(2):
        total0[:, p * part : (p + 1) * part] = products(rows0, 0, p)

    for dz in hops:
        tag(dz, z).wait_send()
    for j in range(1, PLANE):
        tag_side(j, i).wait_send()
    for up in (True, False):
        for d in range(1, half + 1):
            if d < half or up:
                weight_hop(d, up, z).wait_send()
    for c in range(heads):
        for m in range(chips):
            if m:
                weight_chip(c, m, i).wait_send()
            weight_core(c, m, i).wait_send()
    for dx in range(1, heads):
        weight_head(lax.rem(x + dx, heads), x).wait_send()
        rows_head(0, dx, x).wait_send()
    first.finish()
    second.finish()
    for n, block in enumerate((send0, send1, sendq, back0)):
        drain(block, total - 1, a2a_send.at[n])
    receive_back(4, ret1, 1)
    drain(back1, total - 1, a2a_send.at[4])
    rows_gathered(1)
    result = 0.0
    for p in range(2):
        summed = (total0[:, p * part : (p + 1) * part] + products(rows1, cut, p)).astype(BF16)
        result = result + exact(summed, ordered[p * part : (p + 1) * part])
    out_ref[...] = result.astype(BF16)
    for dx in range(1, heads):
        rows_head(1, dx, x).wait_send()


def constants(groups, tokens, quota):
    slots = 2 * groups * quota
    s = np.arange(slots)
    token = np.arange(tokens)
    block = np.arange(groups)
    upto = (token[:, None] <= token[None, :]).astype(np.float32)
    lower = (block[None, :] < block[:, None]).astype(np.float32)
    col = (s[:, None] // (2 * quota) == block[None, :]).astype(np.float32)
    lane = np.arange(LANES)[None, :]
    r, half = (s % quota)[:, None], (s // quota % 2)[:, None]
    masks = []
    for p in range(2):
        masks.append(CSIZE * (lane == r) + 1.0 * (lane == quota + r) - 10000.0 * ((lane == 2 * quota) & (half != p)))
    col_mask = np.stack(masks).astype(np.float32)
    row_mask = np.ascontiguousarray(col_mask.transpose(0, 2, 1))
    as16 = lambda x: jnp.asarray(x, BF16)
    return as16(upto), as16(lower), as16(col), as16(col.T), jnp.asarray(col_mask), jnp.asarray(row_mask)


def column_order(planes, heads, width):
    zs = planes // heads
    each = width // PLANE // zs
    order = np.zeros((width, width), np.float32)
    for p in range(PLANE):
        for zz in range(zs):
            for c in range(each):
                order[(p * zs + zz) * each + c, (zz * PLANE + p) * each + c] = 1.0
    return jnp.asarray(order, BF16)


def layer(picks, location, labels, slot, query, key, value, weight, groups, heads, quota, listed):
    planes = groups // PLANE
    full = planes // 2 - 2
    tokens, features = query.shape
    per_device = tokens // CSIZE
    slots = 2 * groups * quota
    dma = pltpu.SemaphoreType.DMA

    def scratch(*shape):
        return pltpu.VMEM(shape, BF16)

    widths = [heads * HD for heads in GROUPS]
    each = weight.shape[0]
    width = each * groups // heads
    zs = planes // heads
    sends = [scratch(groups, 2 * quota, w) for w in widths + [features // 2]]
    backs = [(groups, 2 * quota, w // 2) for w in widths]
    hots = [scratch(2, slots, tokens), scratch(2, tokens, slots)]
    rings = []
    for w in widths:
        shard, block = (per_device, CSIZE, 2 * w), (CSIZE, 2 * w)
        rings += [scratch(*shard), scratch(groups, *block)]
        rings += [scratch(*shard)] * (2 * full)
        rings += [scratch(2, PLANE + PLANE // 2, *block)] * 2
        rings += [scratch(2, PLANE // 2, *block), scratch(planes * (PLANE - 1), *block)]
        rings += [dma((2, full, SUBS)), dma((2, full, SUBS)), dma((2, 3)), dma((2, 3)), dma, dma]
    return pl.pallas_call(
        functools.partial(layer_kernel, planes, heads, listed),
        out_shape=jax.ShapeDtypeStruct((tokens, width), BF16),
        in_specs=[SMEM, SMEM] + [VMEM] * 14,
        out_specs=VMEM,
        scratch_shapes=sends
        + [scratch(*b) for b in backs]
        + hots
        + sends
        + [
            pltpu.VMEM((PLANE, planes, 1, tokens), labels.dtype),
            pltpu.VMEM((groups, tokens), labels.dtype),
            *hots,
            scratch(per_device, CSIZE, sum(widths)),
        ]
        + [scratch(*b) for b in backs]
        + [scratch(tokens, w) for w in widths]
        + [
            scratch(planes, each, features),
            scratch(PLANE, heads, zs, each, features),
        ]
        + [scratch(heads, tokens, w) for w in widths]
        + [
            pltpu.VMEM((tokens, width), F32),
            dma((2, planes // 2)),
            dma((2, planes // 2)),
            dma((2, heads)),
            *[dma((heads, PLANE // 2))] * 4,
            dma((2, heads)),
            dma((2, heads)),
        ]
        + [dma((5,)), dma((5,)), dma((planes,)), dma((planes,)), dma((PLANE,)), dma((PLANE,))]
        + rings,
        compiler_params=pltpu.CompilerParams(
            collective_id=0, has_side_effects=True, vmem_limit_bytes=61 * 2**20
        ),
        cost_estimate=pl.CostEstimate(flops=2**32, bytes_accessed=2**27, transcendentals=0),
        name="layer",
    )(
        picks,
        location,
        labels.reshape(1, tokens),
        slot.reshape(1, tokens).astype(F32),
        slot.reshape(tokens, 1).astype(F32),
        query,
        key,
        value,
        weight,
        *constants(groups, tokens, quota),
        column_order(planes, heads, width),
    )


def shards(query, key, value, labels, partners, out_weight):
    planes = lax.axis_size("z")
    groups = planes * PLANE
    z, i = lax.axis_index("z"), lax.axis_index("plane")
    device = z * PLANE + i
    tokens, features = query.shape
    per_device = tokens // CSIZE
    listed = partners.shape[1]
    quota = (3 * tokens + 2 * groups - 1) // (2 * groups)

    wanted = partners.reshape(groups, per_device * listed)
    half = planes // 2
    ahead = jnp.array([0] * planes + [2, 1, -2, -1], jnp.int32)
    distance = jnp.array(list(range(planes)) + [half, half - 1, half, half + 1], jnp.int32)
    there = (z + ahead) % planes
    wanting = there[:, None] * PLANE + (i + jnp.arange(PLANE)) % PLANE
    lists = jnp.take(wanted, wanting, axis=0)
    source = ((there - distance) % planes * PLANE + i)[:, None, None]
    picks = jnp.sum(jnp.where(lists // per_device == source, lists - source * per_device, 0), axis=2)
    my_list = lax.dynamic_slice_in_dim(wanted, device, 1, 0)[0]
    from_group = my_list // per_device
    location = (z - from_group // PLANE) % planes * PLANE + from_group % PLANE

    owner = labels // per_device
    before = jnp.arange(tokens)[None, :] < jnp.arange(tokens)[:, None]
    rank = jnp.sum((owner[:, None] == owner[None, :]) & before, axis=1, dtype=jnp.int32)
    slot = owner * (2 * quota) + rank
    return layer(
        picks.reshape(-1).astype(jnp.int32),
        location.astype(jnp.int32),
        labels,
        slot,
        query,
        key,
        value,
        out_weight.T,
        groups,
        lax.axis_size("head"),
        quota,
        listed,
    )


def solution(mesh):
    heads = mesh.shape["head"]
    mesh = jax.sharding.Mesh(mesh.devices.reshape(-1, PLANE, heads), ("z", "plane", "head"))
    clu = ("z", "plane")
    return jax.shard_map(
        shards,
        mesh=mesh,
        in_specs=(
            P(clu, "head"),
            P(clu, "head"),
            P(clu, "head"),
            P(clu),
            P(),
            P("head", clu),
        ),
        out_specs=P(clu, "head"),
        check_vma=False,
    )
```

```python
import functools
import math

import jax
import jax.numpy as jnp
import numpy as np
from jax import lax
from jax.experimental import pallas as pl
from jax.experimental.pallas import tpu as pltpu
from jax.sharding import PartitionSpec as P

HD = 128
CSIZE = 16
PLANE = 8
SUBS = 4
GROUPS = (4, 2)
LANES = 128
MESH = pl.DeviceIdType.MESH
F32 = jnp.float32
BF16 = jnp.bfloat16
VMEM = pl.BlockSpec(memory_space=pltpu.VMEM)
SMEM = pl.BlockSpec(memory_space=pltpu.SMEM)


def drain(ref, count, sem):
    some = ref.at[pl.ds(0, count)]
    pltpu.make_async_copy(some, some, sem).wait()


def exact(a, b):
    return jnp.dot(a, b, preferred_element_type=F32)


class Ring:
    def __init__(self, planes, z, i, pick, kv, out, ups, downs, packs, near, far, stage, sems):
        self.planes, self.half, self.full = planes, planes // 2, planes // 2 - 2
        self.z, self.i = z, i
        self.above = lax.rem(z + 1, planes)
        self.below = lax.rem(z + planes - 1, planes)
        self.pick, self.kv, self.out = pick, kv, out
        self.ups, self.downs = (kv,) + ups, (kv,) + downs
        self.packs, self.near, self.far, self.stage = packs, near, far, stage
        self.ring_send, self.ring_recv, self.pack_send, self.pack_recv, self.side_send, self.side_recv = sems
        self.step = kv.shape[0] // SUBS
        self.part = PLANE // 2

    def send_on(self, src, dst, send, recv, up):
        return pltpu.make_async_remote_copy(
            src_ref=src,
            dst_ref=dst,
            send_sem=send,
            recv_sem=recv,
            device_id={"z": self.above if up else self.below},
            device_id_type=MESH,
        )

    def hop(self, d, s, up):
        held = self.ups if up else self.downs
        rows = pl.ds(s * self.step, self.step)
        n = 0 if up else 1
        return self.send_on(
            held[d - 1].at[rows], held[d].at[rows], self.ring_send.at[n, d - 1, s], self.ring_recv.at[n, d - 1, s], up
        )

    def pack(self, at, up):
        n = 0 if up else 1
        rows = pl.ds(0, self.part) if at == 0 else pl.ds(self.part, PLANE)
        return self.send_on(
            self.packs.at[n, rows], self.near.at[n, rows], self.pack_send.at[n, at], self.pack_recv.at[n, at], up
        )

    def pack_on(self, up):
        n = 0 if up else 1
        return self.send_on(
            self.near.at[n, pl.ds(0, self.part)], self.far.at[n], self.pack_send.at[n, 2], self.pack_recv.at[n, 2], up
        )

    def side(self, k, j, src):
        return pltpu.make_async_remote_copy(
            src_ref=src,
            dst_ref=self.out.at[k * PLANE + self.i],
            send_sem=self.side_send,
            recv_sem=self.side_recv,
            device_id={"plane": lax.rem(self.i + j, PLANE)},
            device_id_type=MESH,
        )

    def spread(self, k, held, these):
        for j in these:
            if j == 0:
                self.out[k * PLANE + self.i] = held[self.pick[k * PLANE]]
            else:
                at = k * (PLANE - 1) + j - 1
                self.stage[at] = held[self.pick[k * PLANE + j]]
                self.side(k, j, self.stage.at[at]).start()

    def pass_out(self, k, j, src):
        if j == 0:
            self.out[k * PLANE + self.i] = src[...]
        else:
            self.side(k, j, src).start()

    def begin(self):
        for s in range(SUBS):
            for up in (True, False):
                self.hop(1, s, up).start()
        self.waiting = [(0, self.kv)]

    def advance(self, d):
        for s in range(SUBS):
            for up in (True, False):
                self.hop(d, s, up).wait_recv()
                if d < self.full:
                    self.hop(d + 1, s, up).start()
            each = PLANE // SUBS
            for k, held in self.waiting:
                self.spread(k, held, range(s * each, (s + 1) * each))
        self.waiting = [(d, self.ups[d]), (self.planes - d, self.downs[d])]
        if d == self.full:
            for up in (True, False):
                n = 0 if up else 1
                held = (self.ups if up else self.downs)[d]
                base = (self.planes + 2 * n) * PLANE
                for j in range(self.part):
                    self.packs[n, j] = held[self.pick[base + n * self.part + j]]
                self.pack(0, up).start()
                for j in range(PLANE):
                    self.packs[n, self.part + j] = held[self.pick[base + PLANE + j]]
                self.pack(1, up).start()
            for k, held in self.waiting:
                self.spread(k, held, range(PLANE))

    def last_hops(self):
        for up in (True, False):
            self.pack(0, up).wait_recv()
            self.pack_on(up).start()
        for up in (True, False):
            n = 0 if up else 1
            self.pack(1, up).wait_recv()
            for j in range(PLANE):
                self.pass_out(self.full + 1 if up else self.planes - self.full - 1, j, self.near.at[n, self.part + j])
        for up in (True, False):
            n = 0 if up else 1
            self.pack_on(up).wait_recv()
            for j in range(self.part):
                self.pass_out(self.half, n * self.part + j, self.far.at[n, j])

    def arrive(self):
        drain(self.out, self.planes * (PLANE - 1), self.side_recv)

    def finish(self):
        for up in (True, False):
            for d in range(1, self.full + 1):
                for s in range(SUBS):
                    self.hop(d, s, up).wait_send()
            self.pack(0, up).wait_send()
            self.pack(1, up).wait_send()
            self.pack_on(up).wait_send()
        drain(self.stage, self.planes * (PLANE - 1), self.side_send)


def attend(listed, first, heads, loc_ref, q_ref, kv_ref, far_ref, o_ref):
    keys = (1 + listed) * CSIZE
    width = heads * HD
    scale = 1.0 / math.sqrt(HD)
    shape = (heads, 2 * CSIZE, 2 * keys)
    row, key = lax.broadcasted_iota(jnp.int32, shape, 1), lax.broadcasted_iota(jnp.int32, shape, 2)
    own = (row >= CSIZE) == (key >= keys)

    def body(pair, carry):
        tiles = []
        for c in (2 * pair, 2 * pair + 1):
            tiles.append((kv_ref, c))
            for p in range(listed):
                tiles.append((far_ref, loc_ref[c * listed + p]))
        scores = []
        for h in range(heads):
            at = (first + h) * HD
            q = jnp.concatenate([q_ref[2 * pair + n, :, at : at + HD] for n in range(2)], axis=0)
            k = jnp.concatenate([ref[at, :, h * HD : (h + 1) * HD] for ref, at in tiles], axis=0)
            scores.append(lax.dot_general(q, k, (((1,), (1,)), ((), ())), preferred_element_type=F32))
        scores = jnp.where(own, jnp.stack(scores) * scale, -jnp.inf)
        powers = jnp.exp(scores - jnp.max(scores, axis=-1, keepdims=True))
        weights = (powers / jnp.sum(powers, axis=-1, keepdims=True)).astype(BF16)
        for h in range(heads):
            v = jnp.concatenate([ref[at, :, width + h * HD : width + (h + 1) * HD] for ref, at in tiles], axis=0)
            o_ref[pl.ds(2 * CSIZE * pair, 2 * CSIZE), h * HD : (h + 1) * HD] = exact(weights[h], v).astype(BF16)
        return carry

    lax.fori_loop(0, q_ref.shape[0] // 2, body, 0)


def layer_kernel(planes, heads, listed, *refs):
    (pick, loc, labels_ref, slot_row, slot_col, query, key, value, weight, *rest) = refs
    (upto, lower, col, row, col_mask, row_mask, ordered, out_ref, *rest) = rest
    (send0, send1, sendq, ret0, ret1, packc, packr, arr0, arr1, arrq, all_ref, lab, dcol, drow, q_ref, back0, back1, o0, o1, *rest) = rest
    (w_ring, w_all, rows0, rows1, total0, w_send, w_recv, w_head, w_chip_send, w_chip_recv, w_core_send, w_core_recv, t_send, t_recv, *rest) = rest
    (a2a_send, a2a_recv, tag_send, tag_recv, tag_side_send, tag_side_recv, *rest) = rest
    per_ring = len(rest) // 2
    z, i = lax.axis_index("z"), lax.axis_index("plane")
    x = lax.axis_index("head")
    me = z * PLANE + i
    half, full, total = planes // 2, planes // 2 - 2, planes * PLANE
    hops = [half]
    for d in range(half - 1, 0, -1):
        hops += [-d, d]

    rings = []
    for g in range(2):
        kv, out, *more = rest[g * per_ring : (g + 1) * per_ring]
        ups, downs, more = tuple(more[:full]), tuple(more[full : 2 * full]), more[2 * full :]
        rings.append(Ring(planes, z, i, pick, kv, out, ups, downs, *more[:4], more[4:]))

    def at(dz, j):
        return lax.rem(z + dz + planes, planes), lax.rem(i + j, PLANE)

    barrier = pltpu.get_barrier_semaphore()

    def greet(r, carry):
        other = lax.rem(me + r, total)
        there = {"z": other // PLANE, "plane": other % PLANE}
        pl.semaphore_signal(barrier, inc=1, device_id=there, device_id_type=MESH)
        return carry

    lax.fori_loop(1, total, greet, 0)
    for dx in range(1, heads):
        pl.semaphore_signal(barrier, inc=1, device_id={"head": lax.rem(x + dx, heads)}, device_id_type=MESH)
    meetings = total + heads - 2

    def to_blocks(hots, upper, lower, block):
        for l in range(0, block.shape[2], LANES):
            part = exact(hots[0], upper(l)) + exact(hots[1], lower(l))
            block[:, :, l : l + LANES] = part.reshape(total, block.shape[1], LANES).astype(BF16)

    def columns(ref, first):
        return lambda l: ref[:, first + l : first + l + LANES]

    slots, tokens = packc.shape[1], packc.shape[2]
    cut = GROUPS[0] * HD
    quota = send0.shape[1] // 2
    for p in range(2):
        number = lax.broadcasted_iota(jnp.int32, (slots, tokens), 0).astype(F32)
        packc[p] = jnp.where(number == slot_row[...] + float(p * quota), 1.0, 0.0).astype(BF16)
    to_blocks(packc, columns(key, 0), columns(value, 0), send0)
    pl.semaphore_wait(barrier, meetings)

    def tag(dz, source):
        return pltpu.make_async_remote_copy(
            src_ref=labels_ref,
            dst_ref=all_ref.at[i, source],
            send_sem=tag_send.at[dz % planes],
            recv_sem=tag_recv.at[source],
            device_id={"z": at(dz, 0)[0]},
            device_id_type=MESH,
        )

    def tag_side(j, source):
        return pltpu.make_async_remote_copy(
            src_ref=all_ref.at[i],
            dst_ref=all_ref.at[source],
            send_sem=tag_side_send.at[j],
            recv_sem=tag_side_recv.at[source],
            device_id={"plane": at(0, j)[1]},
            device_id_type=MESH,
        )

    def exchange(n, block, landed, between=None, halves=(0, 1)):
        def start(to):
            pltpu.make_async_remote_copy(
                src_ref=block.at[to[0] * PLANE + to[1]],
                dst_ref=landed.at[me],
                send_sem=a2a_send.at[n],
                recv_sem=a2a_recv.at[n],
                device_id={"z": to[0], "plane": to[1]},
                device_id_type=MESH,
            ).start()

        def far(j, carry):
            for dz in hops:
                start(at(dz, j))
            return carry

        def close(j, carry):
            start(at(0, j))
            return carry

        if 0 in halves:
            lax.fori_loop(0, PLANE // 2, far, 0)
        if between is not None:
            between()
        if 1 in halves:
            lax.fori_loop(PLANE // 2, PLANE, far, 0)
            lax.fori_loop(1, PLANE, close, 0)
            landed[me] = block[me]

    def landed_all(n, landed):
        drain(landed, total - 1, a2a_recv.at[n])

    def plane_at(d, up):
        return lax.rem(z + planes - d, planes) if up else lax.rem(z + d, planes)

    def weight_hop(d, up, block):
        n = 0 if up else 1
        return pltpu.make_async_remote_copy(
            src_ref=w_ring.at[block],
            dst_ref=w_ring.at[block],
            send_sem=w_send.at[n, d - 1],
            recv_sem=w_recv.at[n, d - 1],
            device_id={"z": plane_at(1, not up)},
            device_id_type=MESH,
        )

    def weight_begins():
        w_ring[z] = weight[...]
        for up in (True, False):
            weight_hop(1, up, z).start()

    def weight_goes_on(d):
        for up in (True, False):
            if d < half or up:
                weight_hop(d, up, plane_at(d, up)).wait_recv()
                if d + 1 < half or (d + 1 == half and up):
                    weight_hop(d + 1, up, plane_at(d, up)).start()

    zs = planes // heads

    def weight_head(to, source):
        return pltpu.make_async_remote_copy(
            src_ref=w_ring.at[pl.ds(to * zs, zs)],
            dst_ref=w_all.at[i, source],
            send_sem=w_head.at[0, to],
            recv_sem=w_head.at[1, source],
            device_id={"head": to},
            device_id_type=MESH,
        )

    chips = PLANE // 2
    sibling = i + 1 - 2 * (i % 2)

    def of_set(c):
        return lax.rem(x + c, heads)

    def weight_chip(c, m, source):
        return pltpu.make_async_remote_copy(
            src_ref=w_all.at[i, of_set(c)],
            dst_ref=w_all.at[source, of_set(c)],
            send_sem=w_chip_send.at[c, m],
            recv_sem=w_chip_recv.at[c, m],
            device_id={"plane": lax.rem(i + 2 * m, PLANE)},
            device_id_type=MESH,
        )

    def weight_core(c, m, first):
        at = lax.rem(first + 2 * m, PLANE)
        return pltpu.make_async_remote_copy(
            src_ref=w_all.at[at, of_set(c)],
            dst_ref=w_all.at[at, of_set(c)],
            send_sem=w_core_send.at[c, m],
            recv_sem=w_core_recv.at[c, m],
            device_id={"plane": sibling},
            device_id_type=MESH,
        )

    def weight_to_chips(c):
        for m in range(1, chips):
            weight_chip(c, m, i).start()
        weight_core(c, 0, i).start()

    def weight_to_core(c):
        for m in range(1, chips):
            weight_chip(c, m, lax.rem(i + PLANE - 2 * m, PLANE)).wait_recv()
        for m in range(1, chips):
            weight_core(c, m, i).start()

    def rows_head(g, dx, source):
        rows = (rows0, rows1)[g]
        return pltpu.make_async_remote_copy(
            src_ref=rows.at[x],
            dst_ref=rows.at[source],
            send_sem=t_send.at[g, dx],
            recv_sem=t_recv.at[g, source],
            device_id={"head": lax.rem(x + dx, heads)},
            device_id_type=MESH,
        )

    def products(rows, first, part):
        width = rows.shape[2]
        held = PLANE // 2
        result = 0.0
        for xx in range(heads):
            block = w_all[part * held : (part + 1) * held, xx, :, :, first : first + width].astype(F32)
            block = block.reshape(block.shape[0] * block.shape[1] * block.shape[2], width).astype(BF16)
            result = result + lax.dot_general(
                rows[xx], block, (((1,), (1,)), ((), ())), preferred_element_type=F32
            )
        return result

    for dz in hops:
        tag(dz, z).start()
    all_ref[i, z] = labels_ref[...]
    weight_begins()
    exchange(0, send0, arr0, lambda: weight_goes_on(1))
    for dz in hops:
        tag(dz, lax.rem(z - dz + planes, planes)).wait_recv()
    for j in range(1, PLANE):
        tag_side(j, i).start()
    to_blocks(packc, columns(key, cut), columns(value, cut), send1)
    weight_goes_on(2)
    exchange(1, send1, arr1)
    to_blocks(packc, columns(query, 0), columns(query, query.shape[1] // 2), sendq)
    weight_goes_on(3)
    exchange(2, sendq, arrq, lambda: weight_goes_on(4))
    for p in range(2):
        number = lax.broadcasted_iota(jnp.int32, (tokens, slots), 1).astype(F32)
        packr[p] = jnp.where(number == slot_col[...] + float(p * quota), 1.0, 0.0).astype(BF16)
    for j in range(1, PLANE):
        tag_side(j, lax.rem(i - j + PLANE, PLANE)).wait_recv()

    for zz in range(planes):
        for ii in range(PLANE):
            lab[zz * PLANE + ii : zz * PLANE + ii + 1, :] = all_ref[ii, zz]
    per_device = q_ref.shape[0]
    local = lab[...] - me * per_device
    mine = jnp.logical_and(local >= 0, local < per_device)
    order = exact(jnp.where(mine, 1.0, 0.0).astype(BF16), upto[...])
    named = jnp.where(mine, (local + 1).astype(F32), 0.0)
    lane = lax.broadcasted_iota(jnp.int32, (total, LANES), 1)
    lanef = lane.astype(F32)
    tags, marks = [], []
    for r in range(quota):
        one = jnp.sum(jnp.where(order == r + 1.0, named, 0.0), axis=1, keepdims=True)
        one = jnp.where(one > 0.0, one - 1.0, -100.0)
        tags.append(one)
        marks.append(jnp.where(lanef == one, 1.0, 0.0))
    earlier = exact(lower[...], sum(marks).astype(BF16))
    table = jnp.where(lane == 2 * quota, 1.0, 0.0)
    for r in range(quota):
        place = jnp.sum(marks[r] * earlier, axis=1, keepdims=True)
        table = jnp.where(lane == r, tags[r], jnp.where(lane == quota + r, place, table))
        earlier = earlier + marks[r]
    wide = exact(col[...], table.astype(BF16))
    tall = exact(table.T.astype(BF16), row[...])
    for p in range(2):
        to = jnp.sum(wide * col_mask[p], axis=1, keepdims=True)
        rows = lax.broadcasted_iota(jnp.int32, (slots, tokens), 1).astype(F32)
        dcol[p] = jnp.where(rows == to, 1.0, 0.0).astype(BF16)
        to = jnp.sum(tall * row_mask[p], axis=0, keepdims=True)
        rows = lax.broadcasted_iota(jnp.int32, (tokens, slots), 0).astype(F32)
        drow[p] = jnp.where(rows == to, 1.0, 0.0).astype(BF16)

    def from_blocks(hots, landed, store):
        width = landed.shape[2]
        for l in range(0, width, LANES):
            block = landed[:, :, l : l + LANES].astype(F32).reshape(slots, LANES).astype(BF16)
            for p in range(2):
                store(p * width + l, exact(hots[p], block).astype(BF16))

    def unpack(landed, target):
        def store(at, part):
            target[:, :, at : at + LANES] = part.reshape(per_device, CSIZE, LANES)

        from_blocks(drow, landed, store)

    def give_back(n, attended, back, ret, halves=(0, 1)):
        to_blocks(dcol, columns(attended, 0), columns(attended, back.shape[2]), back)
        exchange(n, back, ret, None, halves)

    def receive_back(n, ret, g):
        rows = (rows0, rows1)[g]

        def store(at, part):
            rows[x, :, at : at + LANES] = part

        landed_all(n, ret)
        from_blocks(packr, ret, store)
        for dx in range(1, heads):
            rows_head(g, dx, x).start()

    def rows_gathered(g):
        for dx in range(1, heads):
            rows_head(g, dx, lax.rem(x + heads - dx, heads)).wait_recv()

    first, second = rings
    landed_all(0, arr0)
    unpack(arr0, first.kv)
    first.begin()
    weight_goes_on(5)
    for d in range(1, full + 1):
        first.advance(d)
        if d + 5 <= half:
            weight_goes_on(d + 5)
        if d + 5 == half:
            w_all[i, x] = w_ring[pl.ds(x * zs, zs)]
            for dx in range(1, heads):
                weight_head(lax.rem(x + dx, heads), x).start()
            weight_to_chips(0)
        if d + 5 > half:
            c = d + 5 - half
            weight_head(x, of_set(c)).wait_recv()
            weight_to_chips(c)
    landed_all(1, arr1)
    unpack(arr1, second.kv)
    second.begin()
    first.last_hops()
    landed_all(2, arrq)
    unpack(arrq, q_ref)
    second.advance(1)
    weight_to_core(0)
    weight_to_core(1)
    first.arrive()
    attend(listed, 0, GROUPS[0], loc, q_ref, first.kv, first.out, o0)
    second.advance(2)
    give_back(3, o0, back0, ret0, (0,))
    for d in range(3, full + 1):
        second.advance(d)
        if d - 1 < heads:
            weight_to_core(d - 1)
    second.last_hops()
    exchange(3, back0, ret0, None, (1,))
    second.arrive()
    attend(listed, GROUPS[0], GROUPS[1], loc, q_ref, second.kv, second.out, o1)
    give_back(4, o1, back1, ret1)
    receive_back(3, ret0, 0)
    for c in range(heads):
        for m in range(chips):
            weight_core(c, m, sibling).wait_recv()
    rows_gathered(0)
    part = out_ref.shape[1] // 2
    for p in range(2):
        total0[:, p * part : (p + 1) * part] = products(rows0, 0, p)

    for dz in hops:
        tag(dz, z).wait_send()
    for j in range(1, PLANE):
        tag_side(j, i).wait_send()
    for up in (True, False):
        for d in range(1, half + 1):
            if d < half or up:
                weight_hop(d, up, z).wait_send()
    for c in range(heads):
        for m in range(chips):
            if m:
                weight_chip(c, m, i).wait_send()
            weight_core(c, m, i).wait_send()
    for dx in range(1, heads):
        weight_head(lax.rem(x + dx, heads), x).wait_send()
        rows_head(0, dx, x).wait_send()
    first.finish()
    second.finish()
    for n, block in enumerate((send0, send1, sendq, back0)):
        drain(block, total - 1, a2a_send.at[n])
    receive_back(4, ret1, 1)
    drain(back1, total - 1, a2a_send.at[4])
    rows_gathered(1)
    result = 0.0
    for p in range(2):
        summed = (total0[:, p * part : (p + 1) * part] + products(rows1, cut, p)).astype(BF16)
        result = result + exact(summed, ordered[p * part : (p + 1) * part])
    out_ref[...] = result.astype(BF16)
    for dx in range(1, heads):
        rows_head(1, dx, x).wait_send()


def constants(groups, tokens, quota):
    slots = 2 * groups * quota
    s = np.arange(slots)
    token = np.arange(tokens)
    block = np.arange(groups)
    upto = (token[:, None] <= token[None, :]).astype(np.float32)
    lower = (block[None, :] < block[:, None]).astype(np.float32)
    col = (s[:, None] // (2 * quota) == block[None, :]).astype(np.float32)
    lane = np.arange(LANES)[None, :]
    r, half = (s % quota)[:, None], (s // quota % 2)[:, None]
    masks = []
    for p in range(2):
        masks.append(CSIZE * (lane == r) + 1.0 * (lane == quota + r) - 10000.0 * ((lane == 2 * quota) & (half != p)))
    col_mask = np.stack(masks).astype(np.float32)
    row_mask = np.ascontiguousarray(col_mask.transpose(0, 2, 1))
    as16 = lambda x: jnp.asarray(x, BF16)
    return as16(upto), as16(lower), as16(col), as16(col.T), jnp.asarray(col_mask), jnp.asarray(row_mask)


def column_order(planes, heads, width):
    zs = planes // heads
    each = width // PLANE // zs
    order = np.zeros((width, width), np.float32)
    for p in range(PLANE):
        for zz in range(zs):
            for c in range(each):
                order[(p * zs + zz) * each + c, (zz * PLANE + p) * each + c] = 1.0
    return jnp.asarray(order, BF16)


def layer(picks, location, labels, slot, query, key, value, weight, groups, heads, quota, listed):
    planes = groups // PLANE
    full = planes // 2 - 2
    tokens, features = query.shape
    per_device = tokens // CSIZE
    slots = 2 * groups * quota
    dma = pltpu.SemaphoreType.DMA

    def scratch(*shape):
        return pltpu.VMEM(shape, BF16)

    widths = [heads * HD for heads in GROUPS]
    each = weight.shape[0]
    width = each * groups // heads
    zs = planes // heads
    sends = [scratch(groups, 2 * quota, w) for w in widths + [features // 2]]
    backs = [(groups, 2 * quota, w // 2) for w in widths]
    hots = [scratch(2, slots, tokens), scratch(2, tokens, slots)]
    rings = []
    for w in widths:
        shard, block = (per_device, CSIZE, 2 * w), (CSIZE, 2 * w)
        rings += [scratch(*shard), scratch(groups, *block)]
        rings += [scratch(*shard)] * (2 * full)
        rings += [scratch(2, PLANE + PLANE // 2, *block)] * 2
        rings += [scratch(2, PLANE // 2, *block), scratch(planes * (PLANE - 1), *block)]
        rings += [dma((2, full, SUBS)), dma((2, full, SUBS)), dma((2, 3)), dma((2, 3)), dma, dma]
    return pl.pallas_call(
        functools.partial(layer_kernel, planes, heads, listed),
        out_shape=jax.ShapeDtypeStruct((tokens, width), BF16),
        in_specs=[SMEM, SMEM] + [VMEM] * 14,
        out_specs=VMEM,
        scratch_shapes=sends
        + [scratch(*b) for b in backs]
        + hots
        + sends
        + [
            pltpu.VMEM((PLANE, planes, 1, tokens), labels.dtype),
            pltpu.VMEM((groups, tokens), labels.dtype),
            *hots,
            scratch(per_device, CSIZE, sum(widths)),
        ]
        + [scratch(*b) for b in backs]
        + [scratch(tokens, w) for w in widths]
        + [
            scratch(planes, each, features),
            scratch(PLANE, heads, zs, each, features),
        ]
        + [scratch(heads, tokens, w) for w in widths]
        + [
            pltpu.VMEM((tokens, width), F32),
            dma((2, planes // 2)),
            dma((2, planes // 2)),
            dma((2, heads)),
            *[dma((heads, PLANE // 2))] * 4,
            dma((2, heads)),
            dma((2, heads)),
        ]
        + [dma((5,)), dma((5,)), dma((planes,)), dma((planes,)), dma((PLANE,)), dma((PLANE,))]
        + rings,
        compiler_params=pltpu.CompilerParams(
            collective_id=0, has_side_effects=True, vmem_limit_bytes=61 * 2**20
        ),
        cost_estimate=pl.CostEstimate(flops=2**32, bytes_accessed=2**27, transcendentals=0),
        name="layer",
    )(
        picks,
        location,
        labels.reshape(1, tokens),
        slot.reshape(1, tokens).astype(F32),
        slot.reshape(tokens, 1).astype(F32),
        query,
        key,
        value,
        weight,
        *constants(groups, tokens, quota),
        column_order(planes, heads, width),
    )


def shards(query, key, value, labels, partners, out_weight):
    planes = lax.axis_size("z")
    groups = planes * PLANE
    z, i = lax.axis_index("z"), lax.axis_index("plane")
    device = z * PLANE + i
    tokens, features = query.shape
    per_device = tokens // CSIZE
    listed = partners.shape[1]
    quota = (3 * tokens + 2 * groups - 1) // (2 * groups)

    wanted = partners.reshape(groups, per_device * listed)
    half = planes // 2
    ahead = jnp.array([0] * planes + [2, 1, -2, -1], jnp.int32)
    distance = jnp.array(list(range(planes)) + [half, half - 1, half, half + 1], jnp.int32)
    there = (z + ahead) % planes
    wanting = there[:, None] * PLANE + (i + jnp.arange(PLANE)) % PLANE
    lists = jnp.take(wanted, wanting, axis=0)
    source = ((there - distance) % planes * PLANE + i)[:, None, None]
    picks = jnp.sum(jnp.where(lists // per_device == source, lists - source * per_device, 0), axis=2)
    my_list = lax.dynamic_slice_in_dim(wanted, device, 1, 0)[0]
    from_group = my_list // per_device
    location = (z - from_group // PLANE) % planes * PLANE + from_group % PLANE

    owner = labels // per_device
    before = jnp.arange(tokens)[None, :] < jnp.arange(tokens)[:, None]
    rank = jnp.sum((owner[:, None] == owner[None, :]) & before, axis=1, dtype=jnp.int32)
    slot = owner * (2 * quota) + rank
    return layer(
        picks.reshape(-1).astype(jnp.int32),
        location.astype(jnp.int32),
        labels,
        slot,
        query,
        key,
        value,
        out_weight.T,
        groups,
        lax.axis_size("head"),
        quota,
        listed,
    )


def solution(mesh):
    heads = mesh.shape["head"]
    mesh = jax.sharding.Mesh(mesh.devices.reshape(-1, PLANE, heads), ("z", "plane", "head"))
    clu = ("z", "plane")
    return jax.shard_map(
        shards,
        mesh=mesh,
        in_specs=(
            P(clu, "head"),
            P(clu, "head"),
            P(clu, "head"),
            P(clu),
            P(),
            P("head", clu),
        ),
        out_specs=P(clu, "head"),
        check_vma=False,
    )
```

```python
import functools
import math

import jax
import jax.numpy as jnp
import numpy as np
from jax import lax
from jax.experimental import pallas as pl
from jax.experimental.pallas import tpu as pltpu
from jax.sharding import PartitionSpec as P

HD = 128
CSIZE = 16
PLANE = 8
SUBS = 4
GROUPS = (4, 2)
LANES = 128
MESH = pl.DeviceIdType.MESH
F32 = jnp.float32
BF16 = jnp.bfloat16
VMEM = pl.BlockSpec(memory_space=pltpu.VMEM)
SMEM = pl.BlockSpec(memory_space=pltpu.SMEM)


def drain(ref, count, sem):
    some = ref.at[pl.ds(0, count)]
    pltpu.make_async_copy(some, some, sem).wait()


def exact(a, b):
    return jnp.dot(a, b, preferred_element_type=F32)


class Ring:
    def __init__(self, planes, z, i, pick, kv, out, ups, downs, packs, near, far, stage, sems):
        self.planes, self.half, self.full = planes, planes // 2, planes // 2 - 2
        self.z, self.i = z, i
        self.above = lax.rem(z + 1, planes)
        self.below = lax.rem(z + planes - 1, planes)
        self.pick, self.kv, self.out = pick, kv, out
        self.ups, self.downs = (kv,) + ups, (kv,) + downs
        self.packs, self.near, self.far, self.stage = packs, near, far, stage
        self.ring_send, self.ring_recv, self.pack_send, self.pack_recv, self.side_send, self.side_recv = sems
        self.step = kv.shape[0] // SUBS
        self.part = PLANE // 2

    def send_on(self, src, dst, send, recv, up):
        return pltpu.make_async_remote_copy(
            src_ref=src,
            dst_ref=dst,
            send_sem=send,
            recv_sem=recv,
            device_id={"z": self.above if up else self.below},
            device_id_type=MESH,
        )

    def hop(self, d, s, up):
        held = self.ups if up else self.downs
        rows = pl.ds(s * self.step, self.step)
        n = 0 if up else 1
        return self.send_on(
            held[d - 1].at[rows], held[d].at[rows], self.ring_send.at[n, d - 1, s], self.ring_recv.at[n, d - 1, s], up
        )

    def pack(self, at, up):
        n = 0 if up else 1
        rows = pl.ds(0, self.part) if at == 0 else pl.ds(self.part, PLANE)
        return self.send_on(
            self.packs.at[n, rows], self.near.at[n, rows], self.pack_send.at[n, at], self.pack_recv.at[n, at], up
        )

    def pack_on(self, up):
        n = 0 if up else 1
        return self.send_on(
            self.near.at[n, pl.ds(0, self.part)], self.far.at[n], self.pack_send.at[n, 2], self.pack_recv.at[n, 2], up
        )

    def side(self, k, j, src):
        return pltpu.make_async_remote_copy(
            src_ref=src,
            dst_ref=self.out.at[k * PLANE + self.i],
            send_sem=self.side_send,
            recv_sem=self.side_recv,
            device_id={"plane": lax.rem(self.i + j, PLANE)},
            device_id_type=MESH,
        )

    def spread(self, k, held, these):
        for j in these:
            if j == 0:
                self.out[k * PLANE + self.i] = held[self.pick[k * PLANE]]
            else:
                at = k * (PLANE - 1) + j - 1
                self.stage[at] = held[self.pick[k * PLANE + j]]
                self.side(k, j, self.stage.at[at]).start()

    def pass_out(self, k, j, src):
        if j == 0:
            self.out[k * PLANE + self.i] = src[...]
        else:
            self.side(k, j, src).start()

    def begin(self):
        for s in range(SUBS):
            for up in (True, False):
                self.hop(1, s, up).start()
        self.waiting = [(0, self.kv)]

    def advance(self, d):
        for s in range(SUBS):
            for up in (True, False):
                self.hop(d, s, up).wait_recv()
                if d < self.full:
                    self.hop(d + 1, s, up).start()
            each = PLANE // SUBS
            for k, held in self.waiting:
                self.spread(k, held, range(s * each, (s + 1) * each))
        self.waiting = [(d, self.ups[d]), (self.planes - d, self.downs[d])]
        if d == self.full:
            for up in (True, False):
                n = 0 if up else 1
                held = (self.ups if up else self.downs)[d]
                base = (self.planes + 2 * n) * PLANE
                for j in range(self.part):
                    self.packs[n, j] = held[self.pick[base + n * self.part + j]]
                self.pack(0, up).start()
                for j in range(PLANE):
                    self.packs[n, self.part + j] = held[self.pick[base + PLANE + j]]
                self.pack(1, up).start()
            for k, held in self.waiting:
                self.spread(k, held, range(PLANE))

    def last_hops(self):
        for up in (True, False):
            self.pack(0, up).wait_recv()
            self.pack_on(up).start()
        for up in (True, False):
            n = 0 if up else 1
            self.pack(1, up).wait_recv()
            for j in range(PLANE):
                self.pass_out(self.full + 1 if up else self.planes - self.full - 1, j, self.near.at[n, self.part + j])
        for up in (True, False):
            n = 0 if up else 1
            self.pack_on(up).wait_recv()
            for j in range(self.part):
                self.pass_out(self.half, n * self.part + j, self.far.at[n, j])

    def arrive(self):
        drain(self.out, self.planes * (PLANE - 1), self.side_recv)

    def finish(self):
        for up in (True, False):
            for d in range(1, self.full + 1):
                for s in range(SUBS):
                    self.hop(d, s, up).wait_send()
            self.pack(0, up).wait_send()
            self.pack(1, up).wait_send()
            self.pack_on(up).wait_send()
        drain(self.stage, self.planes * (PLANE - 1), self.side_send)


def attend(listed, first, heads, loc_ref, q_ref, kv_ref, far_ref, o_ref):
    keys = (1 + listed) * CSIZE
    width = heads * HD
    scale = 1.0 / math.sqrt(HD)
    shape = (heads, 2 * CSIZE, 2 * keys)
    row, key = lax.broadcasted_iota(jnp.int32, shape, 1), lax.broadcasted_iota(jnp.int32, shape, 2)
    own = (row >= CSIZE) == (key >= keys)

    def body(pair, carry):
        tiles = []
        for c in (2 * pair, 2 * pair + 1):
            tiles.append((kv_ref, c))
            for p in range(listed):
                tiles.append((far_ref, loc_ref[c * listed + p]))
        scores = []
        for h in range(heads):
            at = (first + h) * HD
            q = jnp.concatenate([q_ref[2 * pair + n, :, at : at + HD] for n in range(2)], axis=0)
            k = jnp.concatenate([ref[at, :, h * HD : (h + 1) * HD] for ref, at in tiles], axis=0)
            scores.append(lax.dot_general(q, k, (((1,), (1,)), ((), ())), preferred_element_type=F32))
        scores = jnp.where(own, jnp.stack(scores) * scale, -jnp.inf)
        powers = jnp.exp(scores - jnp.max(scores, axis=-1, keepdims=True))
        weights = (powers / jnp.sum(powers, axis=-1, keepdims=True)).astype(BF16)
        for h in range(heads):
            v = jnp.concatenate([ref[at, :, width + h * HD : width + (h + 1) * HD] for ref, at in tiles], axis=0)
            o_ref[pl.ds(2 * CSIZE * pair, 2 * CSIZE), h * HD : (h + 1) * HD] = exact(weights[h], v).astype(BF16)
        return carry

    lax.fori_loop(0, q_ref.shape[0] // 2, body, 0)


def layer_kernel(planes, heads, listed, *refs):
    (pick, loc, labels_ref, slot_row, slot_col, query, key, value, weight, *rest) = refs
    (upto, lower, col, row, col_mask, row_mask, ordered, out_ref, *rest) = rest
    (send0, send1, sendq, ret0, ret1, packc, packr, arr0, arr1, arrq, all_ref, lab, dcol, drow, q_ref, back0, back1, o0, o1, *rest) = rest
    (w_ring, w_all, rows0, rows1, total0, w_send, w_recv, w_head, w_chip_send, w_chip_recv, w_core_send, w_core_recv, t_send, t_recv, *rest) = rest
    (a2a_send, a2a_recv, tag_send, tag_recv, tag_side_send, tag_side_recv, *rest) = rest
    per_ring = len(rest) // 2
    z, i = lax.axis_index("z"), lax.axis_index("plane")
    x = lax.axis_index("head")
    me = z * PLANE + i
    half, full, total = planes // 2, planes // 2 - 2, planes * PLANE
    hops = [half]
    for d in range(half - 1, 0, -1):
        hops += [-d, d]

    rings = []
    for g in range(2):
        kv, out, *more = rest[g * per_ring : (g + 1) * per_ring]
        ups, downs, more = tuple(more[:full]), tuple(more[full : 2 * full]), more[2 * full :]
        rings.append(Ring(planes, z, i, pick, kv, out, ups, downs, *more[:4], more[4:]))

    def at(dz, j):
        return lax.rem(z + dz + planes, planes), lax.rem(i + j, PLANE)

    barrier = pltpu.get_barrier_semaphore()

    def greet(r, carry):
        other = lax.rem(me + r, total)
        there = {"z": other // PLANE, "plane": other % PLANE}
        pl.semaphore_signal(barrier, inc=1, device_id=there, device_id_type=MESH)
        return carry

    lax.fori_loop(1, total, greet, 0)
    for dx in range(1, heads):
        pl.semaphore_signal(barrier, inc=1, device_id={"head": lax.rem(x + dx, heads)}, device_id_type=MESH)
    meetings = total + heads - 2

    def to_blocks(hots, upper, lower, block):
        for l in range(0, block.shape[2], LANES):
            part = exact(hots[0], upper(l)) + exact(hots[1], lower(l))
            block[:, :, l : l + LANES] = part.reshape(total, block.shape[1], LANES).astype(BF16)

    def columns(ref, first):
        return lambda l: ref[:, first + l : first + l + LANES]

    slots, tokens = packc.shape[1], packc.shape[2]
    cut = GROUPS[0] * HD
    quota = send0.shape[1] // 2
    for p in range(2):
        number = lax.broadcasted_iota(jnp.int32, (slots, tokens), 0).astype(F32)
        packc[p] = jnp.where(number == slot_row[...] + float(p * quota), 1.0, 0.0).astype(BF16)
    to_blocks(packc, columns(key, 0), columns(value, 0), send0)
    pl.semaphore_wait(barrier, meetings)

    def tag(dz, source):
        return pltpu.make_async_remote_copy(
            src_ref=labels_ref,
            dst_ref=all_ref.at[i, source],
            send_sem=tag_send.at[dz % planes],
            recv_sem=tag_recv.at[source],
            device_id={"z": at(dz, 0)[0]},
            device_id_type=MESH,
        )

    def tag_side(j, source):
        return pltpu.make_async_remote_copy(
            src_ref=all_ref.at[i],
            dst_ref=all_ref.at[source],
            send_sem=tag_side_send.at[j],
            recv_sem=tag_side_recv.at[source],
            device_id={"plane": at(0, j)[1]},
            device_id_type=MESH,
        )

    def exchange(n, block, landed, between=None, halves=(0, 1)):
        def start(to):
            pltpu.make_async_remote_copy(
                src_ref=block.at[to[0] * PLANE + to[1]],
                dst_ref=landed.at[me],
                send_sem=a2a_send.at[n],
                recv_sem=a2a_recv.at[n],
                device_id={"z": to[0], "plane": to[1]},
                device_id_type=MESH,
            ).start()

        def far(j, carry):
            for dz in hops:
                start(at(dz, j))
            return carry

        def close(j, carry):
            start(at(0, j))
            return carry

        if 0 in halves:
            lax.fori_loop(0, PLANE // 2, far, 0)
        if between is not None:
            between()
        if 1 in halves:
            lax.fori_loop(PLANE // 2, PLANE, far, 0)
            lax.fori_loop(1, PLANE, close, 0)
            landed[me] = block[me]

    def landed_all(n, landed):
        drain(landed, total - 1, a2a_recv.at[n])

    def plane_at(d, up):
        return lax.rem(z + planes - d, planes) if up else lax.rem(z + d, planes)

    def weight_hop(d, up, block):
        n = 0 if up else 1
        return pltpu.make_async_remote_copy(
            src_ref=w_ring.at[block],
            dst_ref=w_ring.at[block],
            send_sem=w_send.at[n, d - 1],
            recv_sem=w_recv.at[n, d - 1],
            device_id={"z": plane_at(1, not up)},
            device_id_type=MESH,
        )

    def weight_begins():
        w_ring[z] = weight[...]
        for up in (True, False):
            weight_hop(1, up, z).start()

    def weight_goes_on(d):
        for up in (True, False):
            if d < half or up:
                weight_hop(d, up, plane_at(d, up)).wait_recv()
                if d + 1 < half or (d + 1 == half and up):
                    weight_hop(d + 1, up, plane_at(d, up)).start()

    zs = planes // heads

    def weight_head(to, source):
        return pltpu.make_async_remote_copy(
            src_ref=w_ring.at[pl.ds(to * zs, zs)],
            dst_ref=w_all.at[i, source],
            send_sem=w_head.at[0, to],
            recv_sem=w_head.at[1, source],
            device_id={"head": to},
            device_id_type=MESH,
        )

    chips = PLANE // 2
    sibling = i + 1 - 2 * (i % 2)

    def of_set(c):
        return lax.rem(x + c, heads)

    def weight_chip(c, m, source):
        return pltpu.make_async_remote_copy(
            src_ref=w_all.at[i, of_set(c)],
            dst_ref=w_all.at[source, of_set(c)],
            send_sem=w_chip_send.at[c, m],
            recv_sem=w_chip_recv.at[c, m],
            device_id={"plane": lax.rem(i + 2 * m, PLANE)},
            device_id_type=MESH,
        )

    def weight_core(c, m, first):
        at = lax.rem(first + 2 * m, PLANE)
        return pltpu.make_async_remote_copy(
            src_ref=w_all.at[at, of_set(c)],
            dst_ref=w_all.at[at, of_set(c)],
            send_sem=w_core_send.at[c, m],
            recv_sem=w_core_recv.at[c, m],
            device_id={"plane": sibling},
            device_id_type=MESH,
        )

    def weight_to_chips(c):
        for m in range(1, chips):
            weight_chip(c, m, i).start()
        weight_core(c, 0, i).start()

    def weight_to_core(c):
        for m in range(1, chips):
            weight_chip(c, m, lax.rem(i + PLANE - 2 * m, PLANE)).wait_recv()
        for m in range(1, chips):
            weight_core(c, m, i).start()

    def rows_head(g, dx, source):
        rows = (rows0, rows1)[g]
        return pltpu.make_async_remote_copy(
            src_ref=rows.at[x],
            dst_ref=rows.at[source],
            send_sem=t_send.at[g, dx],
            recv_sem=t_recv.at[g, source],
            device_id={"head": lax.rem(x + dx, heads)},
            device_id_type=MESH,
        )

    def products(rows, first, part):
        width = rows.shape[2]
        held = PLANE // 2
        result = 0.0
        for xx in range(heads):
            block = w_all[part * held : (part + 1) * held, xx, :, :, first : first + width].astype(F32)
            block = block.reshape(block.shape[0] * block.shape[1] * block.shape[2], width).astype(BF16)
            result = result + lax.dot_general(
                rows[xx], block, (((1,), (1,)), ((), ())), preferred_element_type=F32
            )
        return result

    for dz in hops:
        tag(dz, z).start()
    all_ref[i, z] = labels_ref[...]
    weight_begins()
    exchange(0, send0, arr0, lambda: weight_goes_on(1))
    for dz in hops:
        tag(dz, lax.rem(z - dz + planes, planes)).wait_recv()
    for j in range(1, PLANE):
        tag_side(j, i).start()
    to_blocks(packc, columns(key, cut), columns(value, cut), send1)
    weight_goes_on(2)
    exchange(1, send1, arr1)
    to_blocks(packc, columns(query, 0), columns(query, query.shape[1] // 2), sendq)
    weight_goes_on(3)
    exchange(2, sendq, arrq, lambda: weight_goes_on(4))
    for p in range(2):
        number = lax.broadcasted_iota(jnp.int32, (tokens, slots), 1).astype(F32)
        packr[p] = jnp.where(number == slot_col[...] + float(p * quota), 1.0, 0.0).astype(BF16)
    for j in range(1, PLANE):
        tag_side(j, lax.rem(i - j + PLANE, PLANE)).wait_recv()

    for zz in range(planes):
        for ii in range(PLANE):
            lab[zz * PLANE + ii : zz * PLANE + ii + 1, :] = all_ref[ii, zz]
    per_device = q_ref.shape[0]
    local = lab[...] - me * per_device
    mine = jnp.logical_and(local >= 0, local < per_device)
    order = exact(jnp.where(mine, 1.0, 0.0).astype(BF16), upto[...])
    named = jnp.where(mine, (local + 1).astype(F32), 0.0)
    lane = lax.broadcasted_iota(jnp.int32, (total, LANES), 1)
    lanef = lane.astype(F32)
    tags, marks = [], []
    for r in range(quota):
        one = jnp.sum(jnp.where(order == r + 1.0, named, 0.0), axis=1, keepdims=True)
        one = jnp.where(one > 0.0, one - 1.0, -100.0)
        tags.append(one)
        marks.append(jnp.where(lanef == one, 1.0, 0.0))
    earlier = exact(lower[...], sum(marks).astype(BF16))
    table = jnp.where(lane == 2 * quota, 1.0, 0.0)
    for r in range(quota):
        place = jnp.sum(marks[r] * earlier, axis=1, keepdims=True)
        table = jnp.where(lane == r, tags[r], jnp.where(lane == quota + r, place, table))
        earlier = earlier + marks[r]
    wide = exact(col[...], table.astype(BF16))
    tall = exact(table.T.astype(BF16), row[...])
    for p in range(2):
        to = jnp.sum(wide * col_mask[p], axis=1, keepdims=True)
        rows = lax.broadcasted_iota(jnp.int32, (slots, tokens), 1).astype(F32)
        dcol[p] = jnp.where(rows == to, 1.0, 0.0).astype(BF16)
        to = jnp.sum(tall * row_mask[p], axis=0, keepdims=True)
        rows = lax.broadcasted_iota(jnp.int32, (tokens, slots), 0).astype(F32)
        drow[p] = jnp.where(rows == to, 1.0, 0.0).astype(BF16)

    def from_blocks(hots, landed, store):
        width = landed.shape[2]
        for l in range(0, width, LANES):
            block = landed[:, :, l : l + LANES].astype(F32).reshape(slots, LANES).astype(BF16)
            for p in range(2):
                store(p * width + l, exact(hots[p], block).astype(BF16))

    def unpack(landed, target):
        def store(at, part):
            target[:, :, at : at + LANES] = part.reshape(per_device, CSIZE, LANES)

        from_blocks(drow, landed, store)

    def give_back(n, attended, back, ret, halves=(0, 1)):
        to_blocks(dcol, columns(attended, 0), columns(attended, back.shape[2]), back)
        exchange(n, back, ret, None, halves)

    def receive_back(n, ret, g):
        rows = (rows0, rows1)[g]

        def store(at, part):
            rows[x, :, at : at + LANES] = part

        landed_all(n, ret)
        from_blocks(packr, ret, store)
        for dx in range(1, heads):
            rows_head(g, dx, x).start()

    def rows_gathered(g):
        for dx in range(1, heads):
            rows_head(g, dx, lax.rem(x + heads - dx, heads)).wait_recv()

    first, second = rings
    landed_all(0, arr0)
    unpack(arr0, first.kv)
    first.begin()
    weight_goes_on(5)
    for d in range(1, full + 1):
        first.advance(d)
        if d + 5 <= half:
            weight_goes_on(d + 5)
        if d + 5 == half:
            w_all[i, x] = w_ring[pl.ds(x * zs, zs)]
            for dx in range(1, heads):
                weight_head(lax.rem(x + dx, heads), x).start()
            weight_to_chips(0)
        if d + 5 > half:
            c = d + 5 - half
            weight_head(x, of_set(c)).wait_recv()
            weight_to_chips(c)
    landed_all(1, arr1)
    unpack(arr1, second.kv)
    second.begin()
    first.last_hops()
    landed_all(2, arrq)
    unpack(arrq, q_ref)
    second.advance(1)
    weight_to_core(0)
    weight_to_core(1)
    first.arrive()
    attend(listed, 0, GROUPS[0], loc, q_ref, first.kv, first.out, o0)
    second.advance(2)
    give_back(3, o0, back0, ret0, (0,))
    for d in range(3, full + 1):
        second.advance(d)
        if d - 1 < heads:
            weight_to_core(d - 1)
    second.last_hops()
    exchange(3, back0, ret0, None, (1,))
    second.arrive()
    attend(listed, GROUPS[0], GROUPS[1], loc, q_ref, second.kv, second.out, o1)
    give_back(4, o1, back1, ret1)
    receive_back(3, ret0, 0)
    receive_back(4, ret1, 1)

    for dz in hops:
        tag(dz, z).wait_send()
    for j in range(1, PLANE):
        tag_side(j, i).wait_send()
    for up in (True, False):
        for d in range(1, half + 1):
            if d < half or up:
                weight_hop(d, up, z).wait_send()
    for c in range(heads):
        for m in range(chips):
            if m:
                weight_chip(c, m, i).wait_send()
            weight_core(c, m, i).wait_send()
    for dx in range(1, heads):
        weight_head(lax.rem(x + dx, heads), x).wait_send()
    first.finish()
    second.finish()
    for n, block in enumerate((send0, send1, sendq, back0)):
        drain(block, total - 1, a2a_send.at[n])
    for c in range(heads):
        for m in range(chips):
            weight_core(c, m, sibling).wait_recv()
    rows_gathered(0)
    part = out_ref.shape[1] // 2
    for p in range(2):
        total0[:, p * part : (p + 1) * part] = products(rows0, 0, p)
    drain(back1, total - 1, a2a_send.at[4])
    rows_gathered(1)
    result = 0.0
    for p in range(2):
        summed = (total0[:, p * part : (p + 1) * part] + products(rows1, cut, p)).astype(BF16)
        result = result + exact(summed, ordered[p * part : (p + 1) * part])
    out_ref[...] = result.astype(BF16)
    for dx in range(1, heads):
        rows_head(0, dx, x).wait_send()
        rows_head(1, dx, x).wait_send()


def constants(groups, tokens, quota):
    slots = 2 * groups * quota
    s = np.arange(slots)
    token = np.arange(tokens)
    block = np.arange(groups)
    upto = (token[:, None] <= token[None, :]).astype(np.float32)
    lower = (block[None, :] < block[:, None]).astype(np.float32)
    col = (s[:, None] // (2 * quota) == block[None, :]).astype(np.float32)
    lane = np.arange(LANES)[None, :]
    r, half = (s % quota)[:, None], (s // quota % 2)[:, None]
    masks = []
    for p in range(2):
        masks.append(CSIZE * (lane == r) + 1.0 * (lane == quota + r) - 10000.0 * ((lane == 2 * quota) & (half != p)))
    col_mask = np.stack(masks).astype(np.float32)
    row_mask = np.ascontiguousarray(col_mask.transpose(0, 2, 1))
    as16 = lambda x: jnp.asarray(x, BF16)
    return as16(upto), as16(lower), as16(col), as16(col.T), jnp.asarray(col_mask), jnp.asarray(row_mask)


def column_order(planes, heads, width):
    zs = planes // heads
    each = width // PLANE // zs
    order = np.zeros((width, width), np.float32)
    for p in range(PLANE):
        for zz in range(zs):
            for c in range(each):
                order[(p * zs + zz) * each + c, (zz * PLANE + p) * each + c] = 1.0
    return jnp.asarray(order, BF16)


def layer(picks, location, labels, slot, query, key, value, weight, groups, heads, quota, listed):
    planes = groups // PLANE
    full = planes // 2 - 2
    tokens, features = query.shape
    per_device = tokens // CSIZE
    slots = 2 * groups * quota
    dma = pltpu.SemaphoreType.DMA

    def scratch(*shape):
        return pltpu.VMEM(shape, BF16)

    widths = [heads * HD for heads in GROUPS]
    each = weight.shape[0]
    width = each * groups // heads
    zs = planes // heads
    sends = [scratch(groups, 2 * quota, w) for w in widths + [features // 2]]
    backs = [(groups, 2 * quota, w // 2) for w in widths]
    hots = [scratch(2, slots, tokens), scratch(2, tokens, slots)]
    rings = []
    for w in widths:
        shard, block = (per_device, CSIZE, 2 * w), (CSIZE, 2 * w)
        rings += [scratch(*shard), scratch(groups, *block)]
        rings += [scratch(*shard)] * (2 * full)
        rings += [scratch(2, PLANE + PLANE // 2, *block)] * 2
        rings += [scratch(2, PLANE // 2, *block), scratch(planes * (PLANE - 1), *block)]
        rings += [dma((2, full, SUBS)), dma((2, full, SUBS)), dma((2, 3)), dma((2, 3)), dma, dma]
    return pl.pallas_call(
        functools.partial(layer_kernel, planes, heads, listed),
        out_shape=jax.ShapeDtypeStruct((tokens, width), BF16),
        in_specs=[SMEM, SMEM] + [VMEM] * 14,
        out_specs=VMEM,
        scratch_shapes=sends
        + [scratch(*b) for b in backs]
        + hots
        + sends
        + [
            pltpu.VMEM((PLANE, planes, 1, tokens), labels.dtype),
            pltpu.VMEM((groups, tokens), labels.dtype),
            *hots,
            scratch(per_device, CSIZE, sum(widths)),
        ]
        + [scratch(*b) for b in backs]
        + [scratch(tokens, w) for w in widths]
        + [
            scratch(planes, each, features),
            scratch(PLANE, heads, zs, each, features),
        ]
        + [scratch(heads, tokens, w) for w in widths]
        + [
            pltpu.VMEM((tokens, width), F32),
            dma((2, planes // 2)),
            dma((2, planes // 2)),
            dma((2, heads)),
            *[dma((heads, PLANE // 2))] * 4,
            dma((2, heads)),
            dma((2, heads)),
        ]
        + [dma((5,)), dma((5,)), dma((planes,)), dma((planes,)), dma((PLANE,)), dma((PLANE,))]
        + rings,
        compiler_params=pltpu.CompilerParams(
            collective_id=0, has_side_effects=True, vmem_limit_bytes=61 * 2**20
        ),
        cost_estimate=pl.CostEstimate(flops=2**32, bytes_accessed=2**27, transcendentals=0),
        name="layer",
    )(
        picks,
        location,
        labels.reshape(1, tokens),
        slot.reshape(1, tokens).astype(F32),
        slot.reshape(tokens, 1).astype(F32),
        query,
        key,
        value,
        weight,
        *constants(groups, tokens, quota),
        column_order(planes, heads, width),
    )


def shards(query, key, value, labels, partners, out_weight):
    planes = lax.axis_size("z")
    groups = planes * PLANE
    z, i = lax.axis_index("z"), lax.axis_index("plane")
    device = z * PLANE + i
    tokens, features = query.shape
    per_device = tokens // CSIZE
    listed = partners.shape[1]
    quota = (3 * tokens + 2 * groups - 1) // (2 * groups)

    wanted = partners.reshape(groups, per_device * listed)
    half = planes // 2
    ahead = jnp.array([0] * planes + [2, 1, -2, -1], jnp.int32)
    distance = jnp.array(list(range(planes)) + [half, half - 1, half, half + 1], jnp.int32)
    there = (z + ahead) % planes
    wanting = there[:, None] * PLANE + (i + jnp.arange(PLANE)) % PLANE
    lists = jnp.take(wanted, wanting, axis=0)
    source = ((there - distance) % planes * PLANE + i)[:, None, None]
    picks = jnp.sum(jnp.where(lists // per_device == source, lists - source * per_device, 0), axis=2)
    my_list = lax.dynamic_slice_in_dim(wanted, device, 1, 0)[0]
    from_group = my_list // per_device
    location = (z - from_group // PLANE) % planes * PLANE + from_group % PLANE

    owner = labels // per_device
    before = jnp.arange(tokens)[None, :] < jnp.arange(tokens)[:, None]
    rank = jnp.sum((owner[:, None] == owner[None, :]) & before, axis=1, dtype=jnp.int32)
    slot = owner * (2 * quota) + rank
    return layer(
        picks.reshape(-1).astype(jnp.int32),
        location.astype(jnp.int32),
        labels,
        slot,
        query,
        key,
        value,
        out_weight.T,
        groups,
        lax.axis_size("head"),
        quota,
        listed,
    )


def solution(mesh):
    heads = mesh.shape["head"]
    mesh = jax.sharding.Mesh(mesh.devices.reshape(-1, PLANE, heads), ("z", "plane", "head"))
    clu = ("z", "plane")
    return jax.shard_map(
        shards,
        mesh=mesh,
        in_specs=(
            P(clu, "head"),
            P(clu, "head"),
            P(clu, "head"),
            P(clu),
            P(),
            P("head", clu),
        ),
        out_specs=P(clu, "head"),
        check_vma=False,
    )
```
